512 devices in a mesh: seq: 64 (over z_lo, y, core), head: 8 (over z_hi, x).
Axes of the slice: x: 4, y: 4, z: 16 (z_hi: 2, z_lo: 8; z = z_hi * 8 + z_lo), core: 2. Of those that a mesh axis runs over, the one named last changes fastest.
Arguments:
- queries: bfloat16 [65536, 2048], P('seq', 'head'), may hold values from -5 to 5
- keys: bfloat16 [65536, 2048], P('seq', 'head'), may hold values from -5 to 5
- values: bfloat16 [65536, 2048], P('seq', 'head'), may hold values from -6.5 to 6.5
- out_grad: bfloat16 [65536, 2048], P('seq', 'head'), may hold values from -6 to 6
Outputs:
- normed: bfloat16 [65536, 2048], P('seq', 'head')
- grad_queries: bfloat16 [65536, 2048], P('seq', 'head')
- grad_keys: bfloat16 [65536, 2048], P('seq', 'head')
- grad_values: bfloat16 [65536, 2048], P('seq', 'head')
- whole_level_grads: float32 [2, 512, 2048], P(None, 'seq', 'head')
The draws below stay inside these ranges and needn't reach their ends.
All inputs are finite; a program needn't handle non-finite values.
Results may differ from the reference program's by a relative error of at most 0.03.
Values may be sent and summed in bfloat16 or wider, within the bound.
No kernel may reach another device: no remote copies, remote signals or barrier semaphores. Data moves between devices by JAX's collectives and lax.ppermute only.
A program may use at most 64 MiB of HBM per device.

```python
import jax
import jax.numpy as jnp
from jax import lax

H = 16
HD = 128
D = 2048
KEPT_PER_SEGMENT = 512
SEQ_LEN = 65536
MIDDLE_SPACING = 8
WHOLE_SPACING = 128


def draw_queries(key, part):
    key = jax.random.fold_in(key, 11)
    drawn = jnp.clip(jax.random.normal(key, (SEQ_LEN, H, HD), jnp.float32), -4.5, 4.5)
    return drawn.reshape(SEQ_LEN, H * HD).astype(jnp.bfloat16)


def draw_keys(key, part):
    key = jax.random.fold_in(key, 12)
    drawn = jnp.clip(jax.random.normal(key, (SEQ_LEN, H, HD), jnp.float32), -4.5, 4.5)
    return drawn.reshape(SEQ_LEN, H * HD).astype(jnp.bfloat16)


def draw_values(key, part):
    key = jax.random.fold_in(key, 13)
    ramp = jnp.arange(H, dtype=jnp.float32)[None, :, None] / (H - 1)
    drawn = jnp.clip(jax.random.normal(key, (SEQ_LEN, H, HD), jnp.float32), -4.0, 4.0) * (0.5 * 3.0 ** ramp)
    return drawn.reshape(SEQ_LEN, H * HD).astype(jnp.bfloat16)


def block_levels(key, shape, cuts, least, top_value):
    def one(position, shards_of):
        steps = jax.random.uniform(jax.random.fold_in(jax.random.fold_in(key, 6), position), (shards_of,), jnp.float32, least / len(cuts), top_value / len(cuts))
        return jnp.repeat(jnp.exp(steps), shape[position] // shards_of).reshape((-1,) + (1,) * (len(shape) - position - 1))

    loudness = one(*cuts[0])
    for cut in cuts[1:]:
        loudness = loudness * one(*cut)
    return loudness


def scatter_about(stream_key, shape, width, most, pieces=(), kind=jnp.bfloat16):
    values = width * jax.random.normal(stream_key, shape, jnp.float32)
    if pieces:
        values = values * block_levels(stream_key, shape, pieces, -0.22, 0.18)
    return jnp.clip(values, -most, most).astype(kind)


def setup_inputs(seed: int = 0) -> dict:
    key_list = jax.random.split(jax.random.key(seed), 5)
    queries = draw_queries(jax.random.fold_in(key_list[4], 71), 0)
    keys = draw_keys(jax.random.fold_in(key_list[4], 71), 0)
    values = draw_values(jax.random.fold_in(key_list[4], 71), 0)
    out_grad = scatter_about(key_list[3], (SEQ_LEN, D), 1.0, 6.0, ((0, 64), (1, 8)))
    return dict(queries=queries, keys=keys, values=values, out_grad=out_grad)


NEG = -1e+30
EPS = 1e-05

def truncated_length(values_in):
    return lax.optimization_barrier(values_in.astype(jnp.bfloat16)).astype(jnp.float32)

def causal_mask(length):
    return jnp.arange(length)[:, None] >= jnp.arange(length)[None, :]

def level_forward(query_matrix, key_matrix, value_matrix):
    multiplier = HD ** (-0.5)
    attention_logits = jnp.einsum('lij,lwj->liw', query_matrix, key_matrix) * multiplier
    attention_logits = jnp.where(causal_mask(KEPT_PER_SEGMENT)[None], attention_logits, NEG)
    row_max = lax.optimization_barrier(jnp.max(attention_logits, axis=-1))
    weight_tensors = jnp.exp(attention_logits - row_max[..., None])
    row_sum = lax.optimization_barrier(jnp.sum(weight_tensors, axis=-1))
    blended_rows = jnp.einsum('hfj,hjr->hfr', truncated_length(weight_tensors), value_matrix)
    return (row_max, row_sum, blended_rows)

def level_backward(query_matrix, key_matrix, value_matrix, row_gradients, log_total, delta_rows):
    multiplier = HD ** (-0.5)
    attention_logits = jnp.einsum('lij,lwj->liw', query_matrix, key_matrix) * multiplier
    attention_logits = jnp.where(causal_mask(KEPT_PER_SEGMENT)[None], attention_logits, NEG)
    softmax_weights = jnp.exp(attention_logits - log_total[..., None])
    probability_gradient = jnp.einsum('lij,lwj->liw', row_gradients, value_matrix)
    logit_gradient = truncated_length(softmax_weights * (probability_gradient - delta_rows[..., None]))
    softmax_weights = truncated_length(softmax_weights)
    query_gradient = jnp.einsum('hfj,hjr->hfr', logit_gradient, key_matrix) * multiplier
    key_gradient = jnp.einsum('uno,unj->uoj', logit_gradient, query_matrix) * multiplier
    value_gradient = jnp.einsum('uno,unj->uoj', softmax_weights, row_gradients)
    return (query_gradient, key_gradient, value_gradient)

def select_rows(row_block, spacing_step, offset):
    grouped = row_block.reshape(SEQ_LEN // spacing_step, spacing_step, HD)
    return lax.dynamic_index_in_dim(grouped, offset, 1, False).reshape(-1, KEPT_PER_SEGMENT, HD)

def select_stat(statistic, spacing_step, offset):
    grouped = statistic.reshape(SEQ_LEN // spacing_step, spacing_step)
    return lax.dynamic_index_in_dim(grouped, offset, 1, False).reshape(-1, KEPT_PER_SEGMENT)

def spread_rows(row_block, spacing_step, offset):
    chosen = (jnp.arange(spacing_step, dtype=jnp.int32) == offset).astype(jnp.float32)
    return (row_block.reshape(-1, 1, HD) * chosen[None, :, None]).reshape(SEQ_LEN, HD)

def spread_stat(statistic, spacing_step, offset, filler):
    chosen = jnp.arange(spacing_step, dtype=jnp.int32) == offset
    return jnp.where(chosen[None, :], statistic.reshape(-1, 1), filler).reshape(SEQ_LEN)

def head_slice(whole, head_id):
    return lax.dynamic_index_in_dim(whole, head_id, 1, False).astype(jnp.float32)

def head_forward(head_id, query_all, key_all, value_all):
    query_head = head_slice(query_all, head_id)
    key_head = head_slice(key_all, head_id)
    value_head = head_slice(value_all, head_id)
    maxima = []
    sums = []
    outputs = []
    for spacing_step in (1, MIDDLE_SPACING, WHOLE_SPACING):
        offset = head_id % spacing_step
        row_max, row_sum, blended_rows = level_forward(select_rows(query_head, spacing_step, offset), select_rows(key_head, spacing_step, offset), select_rows(value_head, spacing_step, offset))
        maxima.append(spread_stat(row_max, spacing_step, offset, NEG))
        sums.append(spread_stat(row_sum, spacing_step, offset, 0.0))
        outputs.append(spread_rows(blended_rows, spacing_step, offset))
    overall_max = jnp.maximum(jnp.maximum(maxima[0], maxima[1]), maxima[2])
    level_scales = [jnp.exp(level_max - overall_max) for level_max in maxima]
    denominator = level_scales[0] * sums[0] + level_scales[1] * sums[1] + level_scales[2] * sums[2]
    merged = (level_scales[0][:, None] * outputs[0] + level_scales[1][:, None] * outputs[1] + level_scales[2][:, None] * outputs[2]) / denominator[:, None]
    return (merged.astype(jnp.bfloat16), overall_max + jnp.log(denominator))

def head_backward(head_id, query_all, key_all, value_all, grad_all, log_totals, deltas):
    query_head = head_slice(query_all, head_id)
    key_head = head_slice(key_all, head_id)
    value_head = head_slice(value_all, head_id)
    grad_head = head_slice(grad_all, head_id)
    log_head = lax.dynamic_index_in_dim(log_totals, head_id, 0, False)
    delta_head = lax.dynamic_index_in_dim(deltas, head_id, 1, False)
    total_dq = jnp.zeros((SEQ_LEN, HD), jnp.float32)
    total_dk = jnp.zeros((SEQ_LEN, HD), jnp.float32)
    total_dv = jnp.zeros((SEQ_LEN, HD), jnp.float32)
    whole_terms = None
    for spacing_step in (1, MIDDLE_SPACING, WHOLE_SPACING):
        offset = head_id % spacing_step
        level_dq, level_dk, level_dv = level_backward(select_rows(query_head, spacing_step, offset), select_rows(key_head, spacing_step, offset), select_rows(value_head, spacing_step, offset), select_rows(grad_head, spacing_step, offset), select_stat(log_head, spacing_step, offset), select_stat(delta_head, spacing_step, offset))
        total_dq = total_dq + spread_rows(level_dq, spacing_step, offset)
        total_dk = total_dk + spread_rows(level_dk, spacing_step, offset)
        total_dv = total_dv + spread_rows(level_dv, spacing_step, offset)
        if spacing_step == WHOLE_SPACING:
            whole_terms = jnp.stack([level_dk[0], level_dv[0]], 0)
    return (total_dq.astype(jnp.bfloat16), total_dk.astype(jnp.bfloat16), total_dv.astype(jnp.bfloat16), whole_terms)

def reference(queries, keys, values, out_grad):
    query_all = queries.reshape(SEQ_LEN, H, HD)
    key_all = keys.reshape(SEQ_LEN, H, HD)
    value_all = values.reshape(SEQ_LEN, H, HD)
    head_numbers = jnp.arange(H, dtype=jnp.int32)
    attention_heads, log_totals = lax.map(lambda head_id: head_forward(head_id, query_all, key_all, value_all), head_numbers)
    attention = attention_heads.transpose(1, 0, 2).reshape(SEQ_LEN, D)
    attention_flat = attention.astype(jnp.float32)
    row_mean = lax.optimization_barrier(jnp.sum(attention_flat, axis=1)) / D
    row_var = lax.optimization_barrier(jnp.sum(attention_flat * attention_flat, axis=1)) / D - row_mean * row_mean
    row_scale = lax.rsqrt(row_var + EPS)
    centred = (attention_flat - row_mean[:, None]) * row_scale[:, None]
    normed = centred.astype(jnp.bfloat16)
    upstream = out_grad.astype(jnp.float32)
    grad_total = lax.optimization_barrier(jnp.sum(upstream, axis=1))
    grad_cross = lax.optimization_barrier(jnp.sum(upstream * centred, axis=1))
    grad_attention = (row_scale[:, None] * (upstream - grad_total[:, None] / D - centred * grad_cross[:, None] / D)).astype(jnp.bfloat16)
    deltas = lax.optimization_barrier(jnp.sum((grad_attention.astype(jnp.float32) * attention_flat).reshape(SEQ_LEN, H, HD), axis=2))
    grad_heads = grad_attention.reshape(SEQ_LEN, H, HD)
    grad_q, grad_k, grad_v, whole_terms = lax.map(lambda head_id: head_backward(head_id, query_all, key_all, value_all, grad_heads, log_totals, deltas), head_numbers)
    return (normed, grad_q.transpose(1, 0, 2).reshape(SEQ_LEN, D), grad_k.transpose(1, 0, 2).reshape(SEQ_LEN, D), grad_v.transpose(1, 0, 2).reshape(SEQ_LEN, D), whole_terms.transpose(1, 2, 0, 3).reshape(2, KEPT_PER_SEGMENT, D))
```

```python
import jax
import jax.numpy as jnp
from jax import lax
from jax.experimental import pallas as pl
from jax.experimental.pallas import tpu as pltpu
from jax.sharding import PartitionSpec as P

H = 16
HD = 128
D = H * HD
TOK = 1024
SEG = 512
NEG = -1e30
EPS = 1e-05
SCALE = HD ** (-0.5)
BF = jnp.bfloat16
F32 = jnp.float32
VMEM = pl.BlockSpec(memory_space=pltpu.VMEM)
SMEM = pl.BlockSpec(memory_space=pltpu.SMEM)
PARAMS = pltpu.CompilerParams(vmem_limit_bytes=16 * 1024 * 1024)


def dot_nt(a, b):
    return lax.dot_general(a, b, (((1,), (1,)), ((), ())), preferred_element_type=F32)


def dot_nn(a, b):
    return lax.dot_general(a, b, (((1,), (0,)), ((), ())), preferred_element_type=F32)


def dot_tn(a, b):
    return lax.dot_general(a, b, (((0,), (0,)), ((), ())), preferred_element_type=F32)


def iota(shape, axis):
    return lax.broadcasted_iota(jnp.int32, shape, axis)


def cost(flops, bytes_accessed, transcendentals=0):
    return pl.CostEstimate(
        flops=flops, bytes_accessed=bytes_accessed, transcendentals=transcendentals
    )


def split3(x):
    hi = x.astype(BF)
    rest = x - hi.astype(F32)
    mid = rest.astype(BF)
    low = (rest - mid.astype(F32)).astype(BF)
    return hi.astype(F32), mid.astype(F32), low.astype(F32)


def select_kernel(idx, q_ref, k_ref, v_ref, mid_ref, far_ref, wide):
    far = []
    for j in range(2):
        head = idx[1] * 2 + j
        for a, ref in enumerate((k_ref, v_ref, q_ref)):
            slot = wide.at[j * 3 + a]
            slot[...] = ref[:, j * HD : (j + 1) * HD].astype(F32)
            mid = slot[pl.ds(lax.rem(head, 8), 128, stride=8), :]
            mid_ref[j * 128 : (j + 1) * 128, a * HD : (a + 1) * HD] = mid.astype(BF)
            far.append(slot[pl.ds(head, 8, stride=128), :])
    for a in range(3):
        both = jnp.concatenate([far[a], far[3 + a]], 0)
        far_ref[:, a * HD : (a + 1) * HD] = both.astype(BF)


def near_forward_kernel(q_ref, k_ref, v_ref, o_ref, lse_ref):
    for c in range(2):
        rows = slice(c * 256, (c + 1) * 256)
        n = (c + 1) * 256
        s = dot_nt(q_ref[rows, :], k_ref[:n, :]) * SCALE
        keep = iota((256, n), 1) <= iota((256, n), 0) + c * 256
        s = jnp.where(keep, s, NEG)
        top = jnp.max(s, axis=1, keepdims=True)
        p = jnp.exp(s - top)
        total = jnp.sum(p, axis=1, keepdims=True)
        o = dot_nn(p.astype(BF), v_ref[:n, :])
        o_ref[0, rows, :] = o / total
        lse_ref[0, rows, :] = jnp.broadcast_to(top + jnp.log(total), (256, HD))


def mid_slots(s, shape, axis):
    n = iota(shape, axis)
    pos = n // 128
    other = s ^ ((pos & 1) * 2 + (pos >> 1))
    return (other & 3) * 128 + (n & 127)


def mid_forward_kernel(idx, mid_ref, o_ref, lse_ref):
    s_idx = idx[0]
    key_slot = mid_slots(s_idx, (128, SEG), 1)
    query_slot = (s_idx & 3) * 128 + iota((128, SEG), 0)
    keep = key_slot <= query_slot
    for j in range(2):
        q = mid_ref[j * 128 : (j + 1) * 128, 2 * HD :]
        k = jnp.concatenate(
            [mid_ref[p * 256 + j * 128 : p * 256 + (j + 1) * 128, :HD] for p in range(4)], 0
        )
        v = jnp.concatenate(
            [mid_ref[p * 256 + j * 128 : p * 256 + (j + 1) * 128, HD : 2 * HD] for p in range(4)], 0
        )
        s = jnp.where(keep, dot_nt(q, k) * SCALE, NEG)
        top = jnp.max(s, axis=1, keepdims=True)
        p = jnp.exp(s - top)
        total = jnp.sum(p, axis=1, keepdims=True)
        o = dot_nn(p.astype(BF), v)
        o_ref[j * 128 : (j + 1) * 128, :] = o / total
        lse_ref[j * 128 : (j + 1) * 128, :] = jnp.broadcast_to(top + jnp.log(total), (128, HD))


def far_places(s):
    n, row = iota((16, 1024), 1), iota((16, 1024), 0)
    pos = n // 16
    flips = (pos & 1) * 32 + (pos & 2) * 8 + (pos & 4) * 2 + ((pos >> 3) & 3) * 2 + (pos >> 5)
    place = (s ^ flips) * 8 + (n & 7)
    return ((n >> 3) & 1) == (row >> 3), place, s * 8 + (row & 7)


def far_keep_forward(s):
    same_head, place, mine = far_places(s)
    return same_head & (place <= mine)


def far_keep_backward(s):
    same_head, place, mine = far_places(s)
    return same_head & (place >= mine)


def pre_kernel(
    idx, o0, lse0, o1, lse1, mid_o, mid_lse, g_ref, att_ref, lse_ref, stat_ref, far_ref, out_scr
):
    for j in range(2):
        head = idx[1] * 2 + j
        picked = pl.ds(lax.rem(head, 8), 128, stride=8)
        distant = pl.ds(head, 8, stride=128)
        own = slice(j * 128, (j + 1) * 128)
        so, sl = out_scr.at[j], lse_ref.at[j]
        so[:SEG, :], so[SEG:, :] = o0[j], o1[j]
        sl[:SEG, :], sl[SEG:, :] = lse0[j], lse1[j]
        l1, l2 = sl[picked, :], mid_lse[own, :]
        peak = jnp.maximum(l1, l2)
        e1, e2 = jnp.exp(l1 - peak), jnp.exp(l2 - peak)
        den = e1 + e2
        so[picked, :] = (e1 * so[picked, :] + e2 * mid_o[own, :]) / den
        sl[picked, :] = peak + jnp.log(den)
        far_ref[0, j * 8 : (j + 1) * 8, :] = so[distant, :]
        far_ref[1, j * 8 : (j + 1) * 8, :] = sl[distant, :]
    lane = iota((128, HD), 1)
    row = iota((128, HD), 0)
    for b in range(8):
        rows = slice(b * 128, (b + 1) * 128)
        at, g = [], []
        for j in range(2):
            a16 = out_scr[j, rows, :].astype(BF)
            att_ref[rows, j * HD : (j + 1) * HD] = a16
            at.append(jnp.where(row == idx[1] * 2 + j, 0.0, a16.astype(F32)))
            g.append(g_ref[rows, j * HD : (j + 1) * HD].astype(F32))
            out_scr[j, rows, :] = g[j]
        sums = (
            at[0] + at[1],
            at[0] * at[0] + at[1] * at[1],
            g[0] * at[0] + g[1] * at[1],
            g[0] + g[1],
        )
        block = jnp.zeros((128, HD), F32)
        for i, term in enumerate(sums):
            block = jnp.where(lane == i, jnp.sum(term, axis=1, keepdims=True), block)
        stat_ref[:, rows] = block.T[:4, :]
    for j in range(2):
        distant = pl.ds(idx[1] * 2 + j, 8, stride=128)
        far_ref[2, j * 8 : (j + 1) * 8, :] = out_scr.at[j][distant, :]


def norm_terms(total, squares, cross, g_total):
    mean = total / D
    rstd = lax.rsqrt(squares / D - mean * mean + EPS)
    return mean, rstd, g_total / D, rstd * (cross - mean * g_total) / D


def stat_pack(lse, delta, lane):
    pack = jnp.zeros(lane.shape, F32)
    for i, term in enumerate(split3(lse) + split3(delta)):
        pack = jnp.where(lane == i, term, pack)
    return pack


def far_forward_kernel(idx, far_all, far_in, stat_in, patch_ref, stat_ref, own_scr):
    s_idx = idx[0]
    q = far_all[:16, 2 * HD :]
    s = jnp.where(far_keep_forward(s_idx), dot_nt(q, far_all[:, :HD]) * SCALE, NEG)
    top = jnp.max(s, axis=1, keepdims=True)
    p = jnp.exp(s - top)
    total = jnp.sum(p, axis=1, keepdims=True)
    o3 = dot_nn(p.astype(BF), far_all[:, HD : 2 * HD]) / total
    l3 = top + jnp.log(total)
    o12, l12, g = far_in[0], far_in[1], far_in[2]
    peak = jnp.maximum(l12, l3)
    e12, e3 = jnp.exp(l12 - peak), jnp.exp(l3 - peak)
    den = e12 + e3
    at = ((e12 * o12 + e3 * o3) / den).astype(BF).astype(F32)
    patch_ref[0] = at
    patch_ref[1] = peak + jnp.log(den)
    lane, row = iota((16, HD), 1), iota((16, HD), 0)
    slot = (row & 7) * 16 + idx[1] * 2 + (row >> 3)
    for k, term in enumerate((at, at * at, g * at)):
        mine = jnp.sum(term, axis=1, keepdims=True)
        own_scr[k : k + 1, :] = jnp.sum(jnp.where(lane == slot, mine, 0.0), axis=0, keepdims=True)
    own_scr[3:4, :] = jnp.zeros((1, HD), F32)
    own = own_scr[...]
    for i in range(8):
        cols = slice(i * 128, (i + 1) * 128)
        mine = jnp.concatenate([own[:, i * 16 : (i + 1) * 16], jnp.zeros((4, HD - 16), F32)], 1)
        stat_ref[:, cols] = stat_in[:, cols] + mine


def far_grad_kernel(idx, stat_ref, far_in, patch_ref, pack_ref, tall_scr, col_scr):
    for i in range(8):
        tall_scr[i * 4 : (i + 1) * 4, :] = stat_ref[:, i * 128 : (i + 1) * 128]
    lane32 = iota((32, HD), 1)
    sums = [[], [], [], []]
    for j in range(2):
        cs = col_scr.at[j]
        chosen = jnp.where(lane32 == idx[1] * 2 + j, tall_scr[...], 0.0)
        cs[...] = jnp.broadcast_to(jnp.sum(chosen, axis=1, keepdims=True), (32, HD))
        for k in range(4):
            sums[k].append(cs[pl.ds(k, 8, stride=4), :])
    mean, rstd, sg, sgx = norm_terms(*(jnp.concatenate(pair, 0) for pair in sums))
    at = patch_ref[0]
    x = (at - mean) * rstd
    grad = (rstd * (far_in[2] - sg - x * sgx)).astype(BF)
    delta = jnp.sum(grad.astype(F32) * at, axis=1, keepdims=True)
    pack_ref[:, :HD] = grad
    delta = jnp.broadcast_to(delta, (16, HD))
    pack_ref[:, HD:] = stat_pack(patch_ref[1], delta, iota((16, HD), 1)).astype(BF)


def norm_kernel(
    idx,
    stat_ref,
    att_ref,
    g_ref,
    lse_in,
    patch_ref,
    normed_ref,
    grad_ref,
    delta_ref,
    lse_ref,
    mid_ref,
    att_scr,
    pack_scr,
):
    for j in range(2):
        distant = pl.ds(idx[1] * 2 + j, 8, stride=128)
        own = slice(j * 8, (j + 1) * 8)
        at, lse = att_scr.at[j], lse_ref.at[j]
        at[...] = att_ref[:, j * HD : (j + 1) * HD].astype(F32)
        at[distant, :] = patch_ref[0, own, :]
        lse[...] = lse_in[j]
        lse[distant, :] = patch_ref[1, own, :]
    lane = iota((128, HD), 1)
    for b in range(8):
        rows = slice(b * 128, (b + 1) * 128)
        stats = stat_ref[:, rows]
        terms = norm_terms(stats[0:1], stats[1:2], stats[2:3], stats[3:4])
        cols = jnp.concatenate(list(terms) + [jnp.zeros((124, HD), F32)], 0).T
        mean, rstd, sg, sgx = (cols[:, i : i + 1] for i in range(4))
        for j in range(2):
            at = att_scr[j, rows, :]
            x = (at - mean) * rstd
            normed_ref[rows, j * HD : (j + 1) * HD] = x.astype(BF)
            g = g_ref[rows, j * HD : (j + 1) * HD].astype(F32)
            grad = (rstd * (g - sg - x * sgx)).astype(BF)
            grad_ref[rows, j * HD : (j + 1) * HD] = grad
            grad = grad.astype(F32)
            delta = jnp.broadcast_to(jnp.sum(grad * at, axis=1, keepdims=True), (128, HD))
            delta_ref[j, rows, :] = delta
            att_scr[j, rows, :] = grad
            pack_scr[j, rows, :] = stat_pack(lse_ref[j, rows, :], delta, lane)
    for j in range(2):
        picked = pl.ds(lax.rem(idx[1] * 2 + j, 8), 128, stride=8)
        mid_ref[j * 128 : (j + 1) * 128, :HD] = att_scr.at[j][picked, :].astype(BF)
        mid_ref[j * 128 : (j + 1) * 128, HD:] = pack_scr.at[j][picked, :].astype(BF)


def near_backward_kernel(
    q_ref, k_ref, v_ref, g_ref, lse_ref, delta_ref, dq_ref, dk_ref, dv_ref
):
    for c in range(2):
        keys = slice(c * 256, (c + 1) * 256)
        rows = slice(c * 256, 512)
        n = 512 - c * 256
        q, g = q_ref[rows, :], g_ref[rows, :]
        k, v = k_ref[keys, :], v_ref[keys, :]
        lse = jnp.concatenate([lse_ref[0, rows, :]] * 2, 1)
        delta = jnp.concatenate([delta_ref[0, rows, :]] * 2, 1)
        s = dot_nt(q, k) * SCALE
        keep = iota((n, 256), 1) <= iota((n, 256), 0)
        p = jnp.exp(jnp.where(keep, s, NEG) - lse)
        ds = (p * (dot_nt(g, v) - delta)).astype(BF)
        p = p.astype(BF)
        dv_ref[0, keys, :] = dot_tn(p, g)
        dk_ref[0, keys, :] = dot_tn(ds, q) * SCALE
        dq = dot_nn(ds, k) * SCALE
        if c == 0:
            dq_ref[0, :, :] = dq
        else:
            dq_ref[0, rows, :] += dq


def query_grad_kernel(idx, dq0, dq1, mid_ref, far_ref, mid_g, far_g, out_ref, scr, far_scr):
    s_idx = idx[0]

    def stat_cols(pack):
        pack = pack.astype(F32)
        lse = pack[:, 0:1] + pack[:, 1:2] + pack[:, 2:3]
        delta = pack[:, 3:4] + pack[:, 4:5] + pack[:, 5:6]
        return lse, delta

    k_all, v_all = far_ref[:, :HD], far_ref[:, HD : 2 * HD]
    lse, delta = stat_cols(far_g[:, HD:])
    s = jnp.where(
        far_keep_forward(s_idx), dot_nt(far_ref[:16, 2 * HD :], k_all) * SCALE, NEG
    )
    p = jnp.exp(s - lse)
    ds = (p * (dot_nt(far_g[:, :HD], v_all) - delta)).astype(BF)
    far_dq = dot_nn(ds, k_all) * SCALE

    key_slot = mid_slots(s_idx, (128, SEG), 1)
    query_slot = (s_idx & 3) * 128 + iota((128, SEG), 0)
    keep = key_slot <= query_slot
    for j in range(2):
        head = idx[1] * 2 + j
        own = slice(j * 128, (j + 1) * 128)
        q = mid_ref[own, 2 * HD :]
        g = mid_g[own, :HD]
        lse, delta = stat_cols(mid_g[own, HD:])
        k = jnp.concatenate(
            [mid_ref[p * 256 + j * 128 : p * 256 + (j + 1) * 128, :HD] for p in range(4)], 0
        )
        v = jnp.concatenate(
            [mid_ref[p * 256 + j * 128 : p * 256 + (j + 1) * 128, HD : 2 * HD] for p in range(4)], 0
        )
        s = jnp.where(keep, dot_nt(q, k) * SCALE, NEG)
        p = jnp.exp(s - lse)
        ds = (p * (dot_nt(g, v) - delta)).astype(BF)
        fs = far_scr.at[j]
        fs[...] = dot_nn(ds, k) * SCALE
        spread = pl.ds(head // 8, 8, stride=16)
        fs[spread, :] = fs[spread, :] + far_dq[j * 8 : (j + 1) * 8]
        picked = pl.ds(lax.rem(head, 8), 128, stride=8)
        sc = scr.at[j]
        sc[:SEG, :], sc[SEG:, :] = dq0[j], dq1[j]
        sc[picked, :] = sc[picked, :] + fs[...]
        out_ref[:, j * HD : (j + 1) * HD] = sc[...].astype(BF)


def key_grad_kernel(
    idx,
    dk0,
    dk1,
    dv0,
    dv1,
    mid_ref,
    far_all,
    grads,
    dk_out,
    dv_out,
    whole_ref,
    scr,
    far_scr,
):
    s_idx = idx[0]
    lane = iota((8, HD), 1)
    row = iota((8, HD), 0)
    pick = ((row == lane // 3) & (lane < 6)).astype(F32).astype(BF)

    far_g = jnp.concatenate([grads[:512, :], grads[1024:1536, :]], 0)
    mid_g = jnp.concatenate([grads[512:1024, :], grads[1536:, :]], 0)
    stats = dot_nt(pick, far_g[:, HD:])
    lse, delta = stats[0:1], stats[1:2]
    keep = far_keep_backward(s_idx)
    k, v = far_all[:16, :HD], far_all[:16, HD : 2 * HD]
    q_all, g_all = far_all[:, 2 * HD :], far_g[:, :HD]
    s = jnp.where(keep, dot_nt(k, q_all) * SCALE, NEG)
    p = jnp.exp(s - lse)
    ds = (p * (dot_nt(v, g_all) - delta)).astype(BF)
    far_dk = dot_nn(ds, q_all) * SCALE
    far_dv = dot_nn(p.astype(BF), g_all)
    for j in range(2):
        whole_ref[0, :, j * HD : (j + 1) * HD] = far_dk[j * 8 : (j + 1) * 8]
        whole_ref[1, :, j * HD : (j + 1) * HD] = far_dv[j * 8 : (j + 1) * 8]

    stats = dot_nt(pick, mid_g[:, HD:])
    query_slot = mid_slots(s_idx, (128, SEG), 1)
    key_slot = (s_idx & 3) * 128 + iota((128, SEG), 0)
    keep = key_slot <= query_slot
    for j in range(2):
        head = idx[1] * 2 + j
        own = slice(j * 128, (j + 1) * 128)
        places = [slice(p * 256 + j * 128, p * 256 + (j + 1) * 128) for p in range(4)]
        k, v = mid_ref[own, :HD], mid_ref[own, HD : 2 * HD]
        q = jnp.concatenate([mid_ref[r, 2 * HD :] for r in places], 0)
        g = jnp.concatenate([mid_g[r, :HD] for r in places], 0)
        lse = jnp.concatenate([stats[0:1, r] for r in places], 1)
        delta = jnp.concatenate([stats[1:2, r] for r in places], 1)
        s = jnp.where(keep, dot_nt(k, q) * SCALE, NEG)
        p = jnp.exp(s - lse)
        ds = (p * (dot_nt(v, g) - delta)).astype(BF)
        mid_dk = dot_nn(ds, q) * SCALE
        mid_dv = dot_nn(p.astype(BF), g)
        spread = pl.ds(head // 8, 8, stride=16)
        picked = pl.ds(lax.rem(head, 8), 128, stride=8)
        for a, (mid, far, near0, near1, out) in enumerate(
            ((mid_dk, far_dk, dk0, dk1, dk_out), (mid_dv, far_dv, dv0, dv1, dv_out))
        ):
            fs, sc = far_scr.at[j * 2 + a], scr.at[j * 2 + a]
            fs[...] = mid
            fs[spread, :] = fs[spread, :] + far[j * 8 : (j + 1) * 8]
            sc[:SEG, :], sc[SEG:, :] = near0[j], near1[j]
            sc[picked, :] = sc[picked, :] + fs[...]
            out[:, j * HD : (j + 1) * HD] = sc[...].astype(BF)


def exchange(x, bit):
    return lax.ppermute(x, "seq", [(i, i ^ bit) for i in range(64)])


def head_exchange(x, bit):
    return lax.ppermute(x, "head", [(i, i ^ bit) for i in range(8)])


def round_of_y(x, to_pair):
    from_far = exchange(x, 4)
    from_pair = exchange(to_pair, 2)
    from_next = exchange(x, 6)
    return from_pair, from_far, from_next


def joined(a, b):
    return jnp.concatenate([a, b], 0)


def after(arrays):
    return lax.optimization_barrier(arrays)


def sds(shape, dtype):
    return jax.ShapeDtypeStruct(shape, dtype)


def local(queries, keys, values, out_grad):
    seq_index = lax.axis_index("seq")
    head_index = lax.axis_index("head")
    idx = jnp.stack([seq_index, head_index]).astype(jnp.int32)

    mid0, far0 = pl.pallas_call(
        select_kernel,
        out_shape=(sds((256, 384), BF), sds((16, 384), BF)),
        in_specs=[SMEM, VMEM, VMEM, VMEM],
        out_specs=(VMEM, VMEM),
        scratch_shapes=[pltpu.VMEM((6, TOK, HD), F32)],
        compiler_params=PARAMS,
        cost_estimate=cost(10**6, 2 * 10**6),
        name="select",
    )(idx, queries, keys, values)

    unit = pl.BlockSpec((SEG, HD), lambda b, j: (b, j))
    by_head = pl.BlockSpec((1, SEG, HD), lambda b, j: (j, b, 0))
    by_head_shape = sds((2, TOK, HD), F32)
    half = pl.BlockSpec((1, SEG, HD), lambda j: (j, 0, 0))
    half_shape = sds((2, SEG, HD), F32)

    def near_forward(block):
        part = pl.BlockSpec((SEG, HD), lambda j: (block, j))
        return pl.pallas_call(
            near_forward_kernel,
            grid=(2,),
            out_shape=(half_shape, half_shape),
            in_specs=[part, part, part],
            out_specs=(half, half),
            compiler_params=PARAMS,
            cost_estimate=cost(4 * 10**8, 2 * 10**6, 10**6),
            name=f"near_forward_{block}",
        )(queries, keys, values)

    mid1 = exchange(mid0, 2)
    far1 = exchange(far0, 32)
    near0 = near_forward(0)
    mid_two, far_two, near0 = after((joined(mid0, mid1), joined(far0, far1), near0))
    mid2 = exchange(mid_two, 1)
    far2 = exchange(far_two, 16)
    near1 = near_forward(1)
    far_four, near1 = after((joined(far_two, far2), near1))
    far4 = exchange(far_four, 8)
    mid_all = joined(mid_two, mid2)
    mid_o, mid_lse = pl.pallas_call(
        mid_forward_kernel,
        out_shape=(sds((256, HD), F32), sds((256, HD), F32)),
        in_specs=[SMEM, VMEM],
        out_specs=(VMEM, VMEM),
        compiler_params=PARAMS,
        cost_estimate=cost(2 * 10**8, 10**6, 10**5),
        name="mid_forward",
    )(idx, mid_all)

    att, lse12, stats, far_in = pl.pallas_call(
        pre_kernel,
        out_shape=(
            sds((TOK, 256), BF),
            by_head_shape,
            sds((4, TOK), F32),
            sds((3, 16, HD), F32),
        ),
        in_specs=[SMEM] + [VMEM] * 7,
        out_specs=(VMEM,) * 4,
        scratch_shapes=[pltpu.VMEM((2, TOK, HD), F32)],
        compiler_params=PARAMS,
        cost_estimate=cost(10**7, 4 * 10**6, 10**5),
        name="pre",
    )(idx, *near0, *near1, mid_o, mid_lse, out_grad)

    far_eight, mid_o = after((joined(far_four, far4), mid_o))
    far_y = [far_eight] + list(round_of_y(far_eight, far_eight))
    far_y, stats = after((jnp.concatenate(far_y, 0), stats))
    far_all = joined(far_y, exchange(far_y, 1))

    patch, stats = pl.pallas_call(
        far_forward_kernel,
        out_shape=(sds((2, 16, HD), F32), sds((4, TOK), F32)),
        in_specs=[SMEM] + [VMEM] * 3,
        out_specs=(VMEM,) * 2,
        scratch_shapes=[pltpu.VMEM((4, HD), F32)],
        compiler_params=PARAMS,
        cost_estimate=cost(10**7, 10**6, 10**5),
        name="far_forward",
    )(idx, far_all, far_in, stats)

    for bit in (2, 1, 4):
        stats = stats + head_exchange(stats, bit)

    far_g = pl.pallas_call(
        far_grad_kernel,
        out_shape=sds((16, 256), BF),
        in_specs=[SMEM] + [VMEM] * 3,
        out_specs=VMEM,
        scratch_shapes=[pltpu.VMEM((32, HD), F32), pltpu.VMEM((2, 32, HD), F32)],
        compiler_params=PARAMS,
        cost_estimate=cost(10**6, 10**5),
        name="far_grad",
    )(idx, stats, far_in, patch)

    stats, far_g = after((stats, far_g))
    part1 = exchange(far_g, 32)
    normed, grad, delta, lse, mid_g = pl.pallas_call(
        norm_kernel,
        out_shape=(
            sds((TOK, 256), BF),
            sds((TOK, 256), BF),
            by_head_shape,
            by_head_shape,
            sds((256, 256), BF),
        ),
        in_specs=[SMEM] + [VMEM] * 5,
        out_specs=(VMEM,) * 5,
        scratch_shapes=[pltpu.VMEM((2, TOK, HD), F32), pltpu.VMEM((2, TOK, HD), F32)],
        compiler_params=PARAMS,
        cost_estimate=cost(10**7, 4 * 10**6),
        name="norm",
    )(idx, stats, att, out_grad, lse12, patch)

    def near_backward(block):
        part = pl.BlockSpec((SEG, HD), lambda j: (block, j))
        stat = pl.BlockSpec((1, SEG, HD), lambda j: (j, block, 0))
        return pl.pallas_call(
            near_backward_kernel,
            grid=(2,),
            out_shape=(half_shape,) * 3,
            in_specs=[part] * 4 + [stat] * 2,
            out_specs=(half,) * 3,
            compiler_params=PARAMS,
            cost_estimate=cost(10**9, 4 * 10**6, 10**6),
            name=f"near_backward_{block}",
        )(queries, keys, values, grad, lse, delta)

    part_a, mid_g = after((joined(far_g, part1), mid_g))
    part2 = exchange(part_a, 16)
    dq0, dk0, dv0 = near_backward(0)
    part_b, dq0 = after((joined(part_a, part2), dq0))
    part3 = exchange(part_b, 8)
    dq1, dk1, dv1 = near_backward(1)
    part_c, dq1 = after((joined(part_b, part3), dq1))
    sent2, sent4, sent6 = round_of_y(part_c, joined(part_c, mid_g))

    grad_queries = pl.pallas_call(
        query_grad_kernel,
        out_shape=sds((TOK, 256), BF),
        in_specs=[SMEM] + [VMEM] * 6,
        out_specs=VMEM,
        scratch_shapes=[pltpu.VMEM((2, TOK, HD), F32), pltpu.VMEM((2, 128, HD), F32)],
        compiler_params=PARAMS,
        cost_estimate=cost(2 * 10**8, 3 * 10**6, 10**5),
        name="query_grad",
    )(idx, dq0, dq1, mid_all, far_all, mid_g, far_g)

    sent = jnp.concatenate([part_c, sent2[:128], sent4, sent6, mid_g, sent2[128:]], 0)
    sent, grad_queries = after((sent, grad_queries))
    grads = joined(sent, exchange(sent, 1))

    grad_keys, grad_values, whole = pl.pallas_call(
        key_grad_kernel,
        out_shape=(sds((TOK, 256), BF), sds((TOK, 256), BF), sds((2, 8, 256), F32)),
        in_specs=[SMEM] + [VMEM] * 7,
        out_specs=(VMEM,) * 3,
        scratch_shapes=[pltpu.VMEM((4, TOK, HD), F32), pltpu.VMEM((4, 128, HD), F32)],
        compiler_params=PARAMS,
        cost_estimate=cost(2 * 10**8, 4 * 10**6, 10**5),
        name="key_grad",
    )(idx, dk0, dk1, dv0, dv1, mid_all, far_all, grads)

    return normed, grad_queries, grad_keys, grad_values, whole


def solution(mesh):
    spec = P("seq", "head")
    return jax.shard_map(
        local,
        mesh=mesh,
        in_specs=(spec,) * 4,
        out_specs=(spec,) * 4 + (P(None, "seq", "head"),),
        check_vma=False,
    )
```

```python
import jax
import jax.numpy as jnp
from jax import lax
from jax.experimental import pallas as pl
from jax.experimental.pallas import tpu as pltpu
from jax.sharding import PartitionSpec as P

H = 16
HD = 128
D = H * HD
TOK = 1024
SEG = 512
NEG = -1e30
EPS = 1e-05
SCALE = HD ** (-0.5)
BF = jnp.bfloat16
F32 = jnp.float32
VMEM = pl.BlockSpec(memory_space=pltpu.VMEM)
SMEM = pl.BlockSpec(memory_space=pltpu.SMEM)
PARAMS = pltpu.CompilerParams(vmem_limit_bytes=16 * 1024 * 1024)


def dot_nt(a, b):
    return lax.dot_general(a, b, (((1,), (1,)), ((), ())), preferred_element_type=F32)


def dot_nn(a, b):
    return lax.dot_general(a, b, (((1,), (0,)), ((), ())), preferred_element_type=F32)


def dot_tn(a, b):
    return lax.dot_general(a, b, (((0,), (0,)), ((), ())), preferred_element_type=F32)


def iota(shape, axis):
    return lax.broadcasted_iota(jnp.int32, shape, axis)


def cost(flops, bytes_accessed, transcendentals=0):
    return pl.CostEstimate(
        flops=flops, bytes_accessed=bytes_accessed, transcendentals=transcendentals
    )


def split3(x):
    hi = x.astype(BF)
    rest = x - hi.astype(F32)
    mid = rest.astype(BF)
    low = (rest - mid.astype(F32)).astype(BF)
    return hi.astype(F32), mid.astype(F32), low.astype(F32)


def select_kernel(idx, q_ref, k_ref, v_ref, mid_ref, far_ref, wide):
    far = []
    for j in range(2):
        head = idx[1] * 2 + j
        for a, ref in enumerate((k_ref, v_ref, q_ref)):
            slot = wide.at[j * 3 + a]
            slot[...] = ref[:, j * HD : (j + 1) * HD].astype(F32)
            mid = slot[pl.ds(lax.rem(head, 8), 128, stride=8), :]
            mid_ref[j * 128 : (j + 1) * 128, a * HD : (a + 1) * HD] = mid.astype(BF)
            far.append(slot[pl.ds(head, 8, stride=128), :])
    for a in range(3):
        both = jnp.concatenate([far[a], far[3 + a]], 0)
        far_ref[:, a * HD : (a + 1) * HD] = both.astype(BF)


def near_forward_kernel(q_ref, k_ref, v_ref, o_ref, lse_ref):
    for c in range(2):
        rows = slice(c * 256, (c + 1) * 256)
        n = (c + 1) * 256
        s = dot_nt(q_ref[rows, :], k_ref[:n, :]) * SCALE
        keep = iota((256, n), 1) <= iota((256, n), 0) + c * 256
        s = jnp.where(keep, s, NEG)
        top = jnp.max(s, axis=1, keepdims=True)
        p = jnp.exp(s - top)
        total = jnp.sum(p, axis=1, keepdims=True)
        o = dot_nn(p.astype(BF), v_ref[:n, :])
        o_ref[0, rows, :] = o / total
        lse_ref[0, rows, :] = jnp.broadcast_to(top + jnp.log(total), (256, HD))


def mid_slots(s, shape, axis):
    n = iota(shape, axis)
    pos = n // 128
    other = s ^ ((pos & 1) * 2 + (pos >> 1))
    return (other & 3) * 128 + (n & 127)


def mid_forward_kernel(idx, mid_ref, o_ref, lse_ref):
    s_idx = idx[0]
    key_slot = mid_slots(s_idx, (128, SEG), 1)
    query_slot = (s_idx & 3) * 128 + iota((128, SEG), 0)
    keep = key_slot <= query_slot
    for j in range(2):
        q = mid_ref[j * 128 : (j + 1) * 128, 2 * HD :]
        k = jnp.concatenate(
            [mid_ref[p * 256 + j * 128 : p * 256 + (j + 1) * 128, :HD] for p in range(4)], 0
        )
        v = jnp.concatenate(
            [mid_ref[p * 256 + j * 128 : p * 256 + (j + 1) * 128, HD : 2 * HD] for p in range(4)], 0
        )
        s = jnp.where(keep, dot_nt(q, k) * SCALE, NEG)
        top = jnp.max(s, axis=1, keepdims=True)
        p = jnp.exp(s - top)
        total = jnp.sum(p, axis=1, keepdims=True)
        o = dot_nn(p.astype(BF), v)
        o_ref[j * 128 : (j + 1) * 128, :] = o / total
        lse_ref[j * 128 : (j + 1) * 128, :] = jnp.broadcast_to(top + jnp.log(total), (128, HD))


def far_places(s):
    n, row = iota((32, 1024), 1), iota((32, 1024), 0)
    pos = n // 32
    flips = (pos & 1) * 32 + (pos & 2) * 8 + (pos & 4) * 2 + ((pos & 8) >> 1) + ((pos & 16) >> 3)
    place = (s ^ flips ^ ((n >> 4) & 1)) * 8 + (n & 7)
    mine = (s ^ (row >> 4)) * 8 + (row & 7)
    return ((n >> 3) & 1) == ((row >> 3) & 1), place, mine


def own_share(idx, keep_ref, reply_ref):
    odd = (iota(keep_ref.shape, 0) * 0 + (idx[0] & 1)) == 1
    return jnp.where(odd, keep_ref[...], reply_ref[...])


def far_keep_forward(s):
    same_head, place, mine = far_places(s)
    return same_head & (place <= mine)


def far_keep_backward(s):
    same_head, place, mine = far_places(s)
    return same_head & (place >= mine)


def pre_kernel(
    idx, o0, lse0, o1, lse1, mid_o, mid_lse, g_ref, att_ref, lse_ref, far_ref, out_scr
):
    for j in range(2):
        head = idx[1] * 2 + j
        picked = pl.ds(lax.rem(head, 8), 128, stride=8)
        distant = pl.ds(head, 8, stride=128)
        own = slice(j * 128, (j + 1) * 128)
        so, sl = out_scr.at[j], lse_ref.at[j]
        so[:SEG, :], so[SEG:, :] = o0[j], o1[j]
        sl[:SEG, :], sl[SEG:, :] = lse0[j], lse1[j]
        l1, l2 = sl[picked, :], mid_lse[own, :]
        peak = jnp.maximum(l1, l2)
        e1, e2 = jnp.exp(l1 - peak), jnp.exp(l2 - peak)
        den = e1 + e2
        so[picked, :] = (e1 * so[picked, :] + e2 * mid_o[own, :]) / den
        sl[picked, :] = peak + jnp.log(den)
        far_ref[j * 8 : (j + 1) * 8, :] = so[distant, :]
        far_ref[16 + j * 8 : 24 + j * 8, :] = sl[distant, :]
    lane = iota((128, HD), 1)
    row = iota((128, HD), 0)
    for b in range(8):
        rows = slice(b * 128, (b + 1) * 128)
        at, g = [], []
        for j in range(2):
            a16 = out_scr[j, rows, :].astype(BF)
            att_ref[rows, j * HD : (j + 1) * HD] = a16
            at.append(jnp.where(row == idx[1] * 2 + j, 0.0, a16.astype(F32)))
            g.append(g_ref[rows, j * HD : (j + 1) * HD].astype(F32))
            out_scr[j, rows, :] = g[j]
        sums = (
            at[0] + at[1],
            at[0] * at[0] + at[1] * at[1],
            g[0] * at[0] + g[1] * at[1],
            g[0] + g[1],
        )
        block = jnp.zeros((128, HD), F32)
        for i, term in enumerate(sums):
            block = jnp.where(lane == i, jnp.sum(term, axis=1, keepdims=True), block)
        far_ref[48 + b * 4 : 52 + b * 4, :] = block.T[:4, :]
    for j in range(2):
        distant = pl.ds(idx[1] * 2 + j, 8, stride=128)
        far_ref[32 + j * 8 : 40 + j * 8, :] = out_scr.at[j][distant, :]


def norm_terms(total, squares, cross, g_total):
    mean = total / D
    rstd = lax.rsqrt(squares / D - mean * mean + EPS)
    return mean, rstd, g_total / D, rstd * (cross - mean * g_total) / D


def stat_pack(lse, delta, lane):
    pack = jnp.zeros(lane.shape, F32)
    for i, term in enumerate(split3(lse) + split3(delta)):
        pack = jnp.where(lane == i, term, pack)
    return pack


def far_forward_kernel(idx, far_all, own_ref, mate_ref, patch_ref, stat_ref):
    q = far_all[:32, 2 * HD :]
    s = jnp.where(far_keep_forward(idx[0]), dot_nt(q, far_all[:, :HD]) * SCALE, NEG)
    top = jnp.max(s, axis=1, keepdims=True)
    p = jnp.exp(s - top)
    total = jnp.sum(p, axis=1, keepdims=True)
    o3 = dot_nn(p.astype(BF), far_all[:, HD : 2 * HD]) / total
    l3 = top + jnp.log(total)
    o12 = jnp.concatenate([own_ref[:16], mate_ref[:16]], 0)
    l12 = jnp.concatenate([own_ref[16:32], mate_ref[16:32]], 0)
    g = jnp.concatenate([own_ref[32:48], mate_ref[32:48]], 0)
    peak = jnp.maximum(l12, l3)
    e12, e3 = jnp.exp(l12 - peak), jnp.exp(l3 - peak)
    den = e12 + e3
    at = ((e12 * o12 + e3 * o3) / den).astype(BF).astype(F32)
    patch_ref[:32] = at
    patch_ref[32:] = peak + jnp.log(den)
    stat_ref[:32, :] = own_ref[48:]
    stat_ref[32:, :] = mate_ref[48:]
    lane, row = iota((32, HD), 1), iota((32, HD), 0)
    here = lane == idx[1] * 2 + ((row >> 3) & 1)
    for k, term in enumerate((at, at * at, g * at)):
        mine = jnp.where(here, jnp.sum(term, axis=1, keepdims=True), 0.0)
        for half in range(2):
            both = mine[half * 16 : half * 16 + 8] + mine[half * 16 + 8 : half * 16 + 16]
            rows = pl.ds(half * 32 + k, 8, stride=4)
            stat_ref[rows, :] = stat_ref[rows, :] + both


def far_grad_kernel(idx, stat_ref, own_ref, mate_ref, patch_ref, pack_ref, col_scr):
    lane64 = iota((64, HD), 1)
    sums = [[], [], [], []]
    for half in range(2):
        for j in range(2):
            cs = col_scr.at[half * 2 + j]
            chosen = jnp.where(lane64 == idx[1] * 2 + j, stat_ref[...], 0.0)
            cs[...] = jnp.broadcast_to(jnp.sum(chosen, axis=1, keepdims=True), (64, HD))
            for k in range(4):
                sums[k].append(cs[pl.ds(half * 32 + k, 8, stride=4), :])
    mean, rstd, sg, sgx = norm_terms(*(jnp.concatenate(part, 0) for part in sums))
    at = patch_ref[:32]
    g = jnp.concatenate([own_ref[32:48], mate_ref[32:48]], 0)
    x = (at - mean) * rstd
    grad = (rstd * (g - sg - x * sgx)).astype(BF)
    delta = jnp.sum(grad.astype(F32) * at, axis=1, keepdims=True)
    pack_ref[:, :HD] = grad
    delta = jnp.broadcast_to(delta, (32, HD))
    pack_ref[:, HD:] = stat_pack(patch_ref[32:], delta, iota((32, HD), 1)).astype(BF)


def stat_cols(pack):
    pack = pack.astype(F32)
    lse = pack[:, 0:1] + pack[:, 1:2] + pack[:, 2:3]
    delta = pack[:, 3:4] + pack[:, 4:5] + pack[:, 5:6]
    return lse, delta


def far_query_kernel(idx, far_all, pack_ref, stat_ref, patch_ref, keep_ref, reply_ref):
    k_all, v_all = far_all[:, :HD], far_all[:, HD : 2 * HD]
    lse, delta = stat_cols(pack_ref[:, HD:])
    keep = far_keep_forward(idx[0])
    s = jnp.where(keep, dot_nt(far_all[:32, 2 * HD :], k_all) * SCALE, NEG)
    p = jnp.exp(s - lse)
    ds = (p * (dot_nt(pack_ref[:, :HD], v_all) - delta)).astype(BF)
    dq = dot_nn(ds, k_all) * SCALE
    for half, out in enumerate((keep_ref, reply_ref)):
        out[:32, :] = stat_ref[half * 32 : half * 32 + 32, :]
        out[32:48, :] = patch_ref[half * 16 : half * 16 + 16, :]
        out[48:64, :] = patch_ref[32 + half * 16 : 48 + half * 16, :]
        out[64:80, :] = dq[half * 16 : half * 16 + 16]


def norm_kernel(
    idx,
    keep_in,
    reply_in,
    att_ref,
    g_ref,
    lse_in,
    normed_ref,
    grad_ref,
    delta_ref,
    lse_ref,
    mid_ref,
    att_scr,
    pack_scr,
):
    share = own_share(idx, keep_in, reply_in)
    for j in range(2):
        distant = pl.ds(idx[1] * 2 + j, 8, stride=128)
        at, lse = att_scr.at[j], lse_ref.at[j]
        at[...] = att_ref[:, j * HD : (j + 1) * HD].astype(F32)
        at[distant, :] = share[32 + j * 8 : 40 + j * 8]
        lse[...] = lse_in[j]
        lse[distant, :] = share[48 + j * 8 : 56 + j * 8]
    lane = iota((128, HD), 1)
    for b in range(8):
        rows = slice(b * 128, (b + 1) * 128)
        stats = share[b * 4 : b * 4 + 4]
        terms = norm_terms(stats[0:1], stats[1:2], stats[2:3], stats[3:4])
        cols = jnp.concatenate(list(terms) + [jnp.zeros((124, HD), F32)], 0).T
        mean, rstd, sg, sgx = (cols[:, i : i + 1] for i in range(4))
        for j in range(2):
            at = att_scr[j, rows, :]
            x = (at - mean) * rstd
            normed_ref[rows, j * HD : (j + 1) * HD] = x.astype(BF)
            g = g_ref[rows, j * HD : (j + 1) * HD].astype(F32)
            grad = (rstd * (g - sg - x * sgx)).astype(BF)
            grad_ref[rows, j * HD : (j + 1) * HD] = grad
            grad = grad.astype(F32)
            delta = jnp.broadcast_to(jnp.sum(grad * at, axis=1, keepdims=True), (128, HD))
            delta_ref[j, rows, :] = delta
            att_scr[j, rows, :] = grad
            pack_scr[j, rows, :] = stat_pack(lse_ref[j, rows, :], delta, lane)
    for j in range(2):
        picked = pl.ds(lax.rem(idx[1] * 2 + j, 8), 128, stride=8)
        mid_ref[j * 128 : (j + 1) * 128, :HD] = att_scr.at[j][picked, :].astype(BF)
        mid_ref[j * 128 : (j + 1) * 128, HD:] = pack_scr.at[j][picked, :].astype(BF)


def near_backward_kernel(
    q_ref, k_ref, v_ref, g_ref, lse_ref, delta_ref, dq_ref, dk_ref, dv_ref
):
    for c in range(2):
        keys = slice(c * 256, (c + 1) * 256)
        rows = slice(c * 256, 512)
        n = 512 - c * 256
        q, g = q_ref[rows, :], g_ref[rows, :]
        k, v = k_ref[keys, :], v_ref[keys, :]
        lse = jnp.concatenate([lse_ref[0, rows, :]] * 2, 1)
        delta = jnp.concatenate([delta_ref[0, rows, :]] * 2, 1)
        s = dot_nt(q, k) * SCALE
        keep = iota((n, 256), 1) <= iota((n, 256), 0)
        p = jnp.exp(jnp.where(keep, s, NEG) - lse)
        ds = (p * (dot_nt(g, v) - delta)).astype(BF)
        p = p.astype(BF)
        dv_ref[0, keys, :] = dot_tn(p, g)
        dk_ref[0, keys, :] = dot_tn(ds, q) * SCALE
        dq = dot_nn(ds, k) * SCALE
        if c == 0:
            dq_ref[0, :, :] = dq
        else:
            dq_ref[0, rows, :] += dq


def query_grad_kernel(idx, dq0, dq1, mid_ref, mid_g, keep_in, reply_in, out_ref, scr, far_scr):
    s_idx = idx[0]
    far_dq = own_share(idx, keep_in, reply_in)[64:80]
    key_slot = mid_slots(s_idx, (128, SEG), 1)
    query_slot = (s_idx & 3) * 128 + iota((128, SEG), 0)
    keep = key_slot <= query_slot
    for j in range(2):
        head = idx[1] * 2 + j
        own = slice(j * 128, (j + 1) * 128)
        q = mid_ref[own, 2 * HD :]
        g = mid_g[own, :HD]
        lse, delta = stat_cols(mid_g[own, HD:])
        k = jnp.concatenate(
            [mid_ref[p * 256 + j * 128 : p * 256 + (j + 1) * 128, :HD] for p in range(4)], 0
        )
        v = jnp.concatenate(
            [mid_ref[p * 256 + j * 128 : p * 256 + (j + 1) * 128, HD : 2 * HD] for p in range(4)], 0
        )
        s = jnp.where(keep, dot_nt(q, k) * SCALE, NEG)
        p = jnp.exp(s - lse)
        ds = (p * (dot_nt(g, v) - delta)).astype(BF)
        fs = far_scr.at[j]
        fs[...] = dot_nn(ds, k) * SCALE
        spread = pl.ds(head // 8, 8, stride=16)
        fs[spread, :] = fs[spread, :] + far_dq[j * 8 : (j + 1) * 8]
        picked = pl.ds(lax.rem(head, 8), 128, stride=8)
        sc = scr.at[j]
        sc[:SEG, :], sc[SEG:, :] = dq0[j], dq1[j]
        sc[picked, :] = sc[picked, :] + fs[...]
        out_ref[:, j * HD : (j + 1) * HD] = sc[...].astype(BF)


def stat_rows(packs):
    lane, row = iota((8, HD), 1), iota((8, HD), 0)
    pick = ((row == lane // 3) & (lane < 6)).astype(F32).astype(BF)
    stats = dot_nt(pick, packs)
    return stats[0:1], stats[1:2]


def far_key_kernel(idx, far_all, grads, keep_ref, reply_ref):
    lse, delta = stat_rows(grads[:, HD:])
    k, v = far_all[:32, :HD], far_all[:32, HD : 2 * HD]
    q_all, g_all = far_all[:, 2 * HD :], grads[:, :HD]
    s = jnp.where(far_keep_backward(idx[0]), dot_nt(k, q_all) * SCALE, NEG)
    p = jnp.exp(s - lse)
    ds = (p * (dot_nt(v, g_all) - delta)).astype(BF)
    dk = dot_nn(ds, q_all) * SCALE
    dv = dot_nn(p.astype(BF), g_all)
    for half, out in enumerate((keep_ref, reply_ref)):
        out[:16, :] = dk[half * 16 : half * 16 + 16]
        out[16:, :] = dv[half * 16 : half * 16 + 16]


def mid_key_kernel(idx, dk0, dk1, dv0, dv1, mid_ref, grads, dk_ref, dv_ref):
    s_idx = idx[0]
    all_lse, all_delta = stat_rows(grads[:, HD:])
    query_slot = mid_slots(s_idx, (128, SEG), 1)
    key_slot = (s_idx & 3) * 128 + iota((128, SEG), 0)
    keep = key_slot <= query_slot
    for j in range(2):
        own = slice(j * 128, (j + 1) * 128)
        places = [slice(p * 256 + j * 128, p * 256 + (j + 1) * 128) for p in range(4)]
        k, v = mid_ref[own, :HD], mid_ref[own, HD : 2 * HD]
        q = jnp.concatenate([mid_ref[r, 2 * HD :] for r in places], 0)
        g = jnp.concatenate([grads[r, :HD] for r in places], 0)
        lse = jnp.concatenate([all_lse[:, r] for r in places], 1)
        delta = jnp.concatenate([all_delta[:, r] for r in places], 1)
        s = jnp.where(keep, dot_nt(k, q) * SCALE, NEG)
        p = jnp.exp(s - lse)
        ds = (p * (dot_nt(v, g) - delta)).astype(BF)
        picked = pl.ds(lax.rem(idx[1] * 2 + j, 8), 128, stride=8)
        for near0, near1, mid, out_ref in (
            (dk0, dk1, dot_nn(ds, q) * SCALE, dk_ref),
            (dv0, dv1, dot_nn(p.astype(BF), g), dv_ref),
        ):
            out = out_ref.at[j]
            out[:SEG, :], out[SEG:, :] = near0[j], near1[j]
            out[picked, :] = out[picked, :] + mid


def key_grad_kernel(idx, dk_in, dv_in, keep_in, reply_in, dk_out, dv_out, whole_ref, scr):
    share = own_share(idx, keep_in, reply_in)
    for j in range(2):
        distant = pl.ds(idx[1] * 2 + j, 8, stride=128)
        for a, (near, out) in enumerate(((dk_in, dk_out), (dv_in, dv_out))):
            far = share[a * 16 + j * 8 : a * 16 + j * 8 + 8]
            whole_ref[a, :, j * HD : (j + 1) * HD] = far
            sc = scr.at[j * 2 + a]
            sc[...] = near[j]
            sc[distant, :] = sc[distant, :] + far
            out[:, j * HD : (j + 1) * HD] = sc[...].astype(BF)


def exchange(x, bit):
    return lax.ppermute(x, "seq", [(i, i ^ bit) for i in range(64)])


def odd_exchange(x, bit):
    return lax.ppermute(x, "seq", [(i, i ^ bit) for i in range(1, 64, 2)])


def odd_head_exchange(x, bit):
    pairs = [(s * 8 + h, s * 8 + (h ^ bit)) for s in range(1, 64, 2) for h in range(8)]
    return lax.ppermute(x, ("seq", "head"), pairs)


def to_odd(x):
    return lax.ppermute(x, "seq", [(i, i + 1) for i in range(0, 64, 2)])


def to_even(x):
    return lax.ppermute(x, "seq", [(i + 1, i) for i in range(0, 64, 2)])


def joined(a, b):
    return jnp.concatenate([a, b], 0)


def after(arrays):
    return lax.optimization_barrier(arrays)


def sds(shape, dtype):
    return jax.ShapeDtypeStruct(shape, dtype)


def local(queries, keys, values, out_grad):
    seq_index = lax.axis_index("seq")
    head_index = lax.axis_index("head")
    idx = jnp.stack([seq_index, head_index]).astype(jnp.int32)

    mid0, far0 = pl.pallas_call(
        select_kernel,
        out_shape=(sds((256, 384), BF), sds((16, 384), BF)),
        in_specs=[SMEM, VMEM, VMEM, VMEM],
        out_specs=(VMEM, VMEM),
        scratch_shapes=[pltpu.VMEM((6, TOK, HD), F32)],
        compiler_params=PARAMS,
        cost_estimate=cost(10**6, 2 * 10**6),
        name="select",
    )(idx, queries, keys, values)

    unit = pl.BlockSpec((SEG, HD), lambda b, j: (b, j))
    by_head = pl.BlockSpec((1, SEG, HD), lambda b, j: (j, b, 0))
    by_head_shape = sds((2, TOK, HD), F32)
    half = pl.BlockSpec((1, SEG, HD), lambda j: (j, 0, 0))
    half_shape = sds((2, SEG, HD), F32)

    def near_forward(block):
        part = pl.BlockSpec((SEG, HD), lambda j: (block, j))
        return pl.pallas_call(
            near_forward_kernel,
            grid=(2,),
            out_shape=(half_shape, half_shape),
            in_specs=[part, part, part],
            out_specs=(half, half),
            compiler_params=PARAMS,
            cost_estimate=cost(4 * 10**8, 2 * 10**6, 10**6),
            name=f"near_forward_{block}",
        )(queries, keys, values)

    mate_far = to_odd(far0)
    mid1 = exchange(mid0, 2)
    far1 = joined(far0, mate_far)
    from1 = odd_exchange(far1, 32)
    near0 = near_forward(0)
    mid_two, far2, near0 = after((joined(mid0, mid1), joined(far1, from1), near0))
    mid2 = exchange(mid_two, 1)
    from2 = odd_exchange(far2, 16)
    near1 = near_forward(1)
    far4, near1 = after((joined(far2, from2), near1))
    from4 = odd_exchange(far4, 8)
    mid_all = joined(mid_two, mid2)
    mid_o, mid_lse = pl.pallas_call(
        mid_forward_kernel,
        out_shape=(sds((256, HD), F32), sds((256, HD), F32)),
        in_specs=[SMEM, VMEM],
        out_specs=(VMEM, VMEM),
        compiler_params=PARAMS,
        cost_estimate=cost(2 * 10**8, 10**6, 10**5),
        name="mid_forward",
    )(idx, mid_all)

    far8, mid_o = after((joined(far4, from4), mid_o))
    from8 = odd_exchange(far8, 4)
    att, lse12, bundle = pl.pallas_call(
        pre_kernel,
        out_shape=(sds((TOK, 256), BF), by_head_shape, sds((80, HD), F32)),
        in_specs=[SMEM] + [VMEM] * 7,
        out_specs=(VMEM,) * 3,
        scratch_shapes=[pltpu.VMEM((2, TOK, HD), F32)],
        compiler_params=PARAMS,
        cost_estimate=cost(10**7, 4 * 10**6, 10**5),
        name="pre",
    )(idx, *near0, *near1, mid_o, mid_lse, out_grad)
    far16, bundle = after((joined(far8, from8), bundle))
    from16 = odd_exchange(far16, 2)
    mate_bundle = to_odd(bundle)
    far_all = joined(far16, from16)

    patch, stats = pl.pallas_call(
        far_forward_kernel,
        out_shape=(sds((64, HD), F32), sds((64, HD), F32)),
        in_specs=[SMEM] + [VMEM] * 3,
        out_specs=(VMEM,) * 2,
        compiler_params=PARAMS,
        cost_estimate=cost(10**7, 10**6, 10**5),
        name="far_forward",
    )(idx, far_all, bundle, mate_bundle)

    for bit in (2, 1, 4):
        stats = stats + odd_head_exchange(stats, bit)

    far_g = pl.pallas_call(
        far_grad_kernel,
        out_shape=sds((32, 256), BF),
        in_specs=[SMEM] + [VMEM] * 4,
        out_specs=VMEM,
        scratch_shapes=[pltpu.VMEM((4, 64, HD), F32)],
        compiler_params=PARAMS,
        cost_estimate=cost(10**6, 10**5),
        name="far_grad",
    )(idx, stats, bundle, mate_bundle, patch)

    part1 = odd_exchange(far_g, 32)
    keep, reply = pl.pallas_call(
        far_query_kernel,
        out_shape=(sds((80, HD), F32), sds((80, HD), F32)),
        in_specs=[SMEM] + [VMEM] * 4,
        out_specs=(VMEM,) * 2,
        compiler_params=PARAMS,
        cost_estimate=cost(10**7, 10**6, 10**5),
        name="far_query",
    )(idx, far_all, far_g, stats, patch)
    reply = to_even(reply)
    normed, grad, delta, lse, mid_g = pl.pallas_call(
        norm_kernel,
        out_shape=(
            sds((TOK, 256), BF),
            sds((TOK, 256), BF),
            by_head_shape,
            by_head_shape,
            sds((256, 256), BF),
        ),
        in_specs=[SMEM] + [VMEM] * 5,
        out_specs=(VMEM,) * 5,
        scratch_shapes=[pltpu.VMEM((2, TOK, HD), F32), pltpu.VMEM((2, TOK, HD), F32)],
        compiler_params=PARAMS,
        cost_estimate=cost(10**7, 4 * 10**6),
        name="norm",
    )(idx, keep, reply, att, out_grad, lse12)

    def near_backward(block):
        part = pl.BlockSpec((SEG, HD), lambda j: (block, j))
        stat = pl.BlockSpec((1, SEG, HD), lambda j: (j, block, 0))
        return pl.pallas_call(
            near_backward_kernel,
            grid=(2,),
            out_shape=(half_shape,) * 3,
            in_specs=[part] * 4 + [stat] * 2,
            out_specs=(half,) * 3,
            compiler_params=PARAMS,
            cost_estimate=cost(10**9, 4 * 10**6, 10**6),
            name=f"near_backward_{block}",
        )(queries, keys, values, grad, lse, delta)

    part_a, mid_g = after((joined(far_g, part1), mid_g))
    part2 = odd_exchange(part_a, 16)
    mid_g1 = exchange(mid_g, 2)
    dq0, dk0, dv0 = near_backward(0)
    part_b, dq0 = after((joined(part_a, part2), dq0))
    part3 = odd_exchange(part_b, 8)
    dq1, dk1, dv1 = near_backward(1)
    part_c, mid_gs, dq1 = after((joined(part_b, part3), joined(mid_g, mid_g1), dq1))
    part4 = odd_exchange(part_c, 4)
    mid_g2 = exchange(mid_gs, 1)

    grad_queries = pl.pallas_call(
        query_grad_kernel,
        out_shape=sds((TOK, 256), BF),
        in_specs=[SMEM] + [VMEM] * 6,
        out_specs=VMEM,
        scratch_shapes=[pltpu.VMEM((2, TOK, HD), F32), pltpu.VMEM((2, 128, HD), F32)],
        compiler_params=PARAMS,
        cost_estimate=cost(2 * 10**8, 3 * 10**6, 10**5),
        name="query_grad",
    )(idx, dq0, dq1, mid_all, mid_g, keep, reply)

    part_d, grad_queries = after((joined(part_c, part4), grad_queries))
    part5 = odd_exchange(part_d, 2)
    dk, dv = pl.pallas_call(
        mid_key_kernel,
        out_shape=(by_head_shape, by_head_shape),
        in_specs=[SMEM] + [VMEM] * 6,
        out_specs=(VMEM,) * 2,
        compiler_params=PARAMS,
        cost_estimate=cost(2 * 10**8, 4 * 10**6, 10**5),
        name="mid_key",
    )(idx, dk0, dk1, dv0, dv1, mid_all, joined(mid_gs, mid_g2))
    far_gs, dk = after((joined(part_d, part5), dk))

    keep, reply = pl.pallas_call(
        far_key_kernel,
        out_shape=(sds((32, HD), F32), sds((32, HD), F32)),
        in_specs=[SMEM] + [VMEM] * 2,
        out_specs=(VMEM,) * 2,
        compiler_params=PARAMS,
        cost_estimate=cost(10**7, 10**6, 10**5),
        name="far_key",
    )(idx, far_all, far_gs)

    grad_keys, grad_values, whole = pl.pallas_call(
        key_grad_kernel,
        out_shape=(sds((TOK, 256), BF), sds((TOK, 256), BF), sds((2, 8, 256), F32)),
        in_specs=[SMEM] + [VMEM] * 4,
        out_specs=(VMEM,) * 3,
        scratch_shapes=[pltpu.VMEM((4, TOK, HD), F32)],
        compiler_params=PARAMS,
        cost_estimate=cost(10**6, 4 * 10**6),
        name="key_grad",
    )(idx, dk, dv, keep, to_even(reply))

    return normed, grad_queries, grad_keys, grad_values, whole


def solution(mesh):
    spec = P("seq", "head")
    return jax.shard_map(
        local,
        mesh=mesh,
        in_specs=(spec,) * 4,
        out_specs=(spec,) * 4 + (P(None, "seq", "head"),),
        check_vma=False,
    )
```

```python
import jax
import jax.numpy as jnp
from jax import lax
from jax.experimental import pallas as pl
from jax.experimental.pallas import tpu as pltpu
from jax.sharding import PartitionSpec as P

H = 16
HD = 128
D = H * HD
TOK = 1024
SEG = 512
NEG = -1e30
EPS = 1e-05
SCALE = HD ** (-0.5)
BF = jnp.bfloat16
F32 = jnp.float32
VMEM = pl.BlockSpec(memory_space=pltpu.VMEM)
SMEM = pl.BlockSpec(memory_space=pltpu.SMEM)
PARAMS = pltpu.CompilerParams(vmem_limit_bytes=16 * 1024 * 1024)


def dot_nt(a, b):
    return lax.dot_general(a, b, (((1,), (1,)), ((), ())), preferred_element_type=F32)


def dot_nn(a, b):
    return lax.dot_general(a, b, (((1,), (0,)), ((), ())), preferred_element_type=F32)


def dot_tn(a, b):
    return lax.dot_general(a, b, (((0,), (0,)), ((), ())), preferred_element_type=F32)


def iota(shape, axis):
    return lax.broadcasted_iota(jnp.int32, shape, axis)


def cost(flops, bytes_accessed, transcendentals=0):
    return pl.CostEstimate(
        flops=flops, bytes_accessed=bytes_accessed, transcendentals=transcendentals
    )


def split3(x):
    hi = x.astype(BF)
    rest = x - hi.astype(F32)
    mid = rest.astype(BF)
    low = (rest - mid.astype(F32)).astype(BF)
    return hi.astype(F32), mid.astype(F32), low.astype(F32)


def select_kernel(idx, q_ref, k_ref, v_ref, mid_ref, far_ref, wide):
    far = []
    for j in range(2):
        head = idx[1] * 2 + j
        for a, ref in enumerate((k_ref, v_ref, q_ref)):
            slot = wide.at[j * 3 + a]
            slot[...] = ref[:, j * HD : (j + 1) * HD].astype(F32)
            mid = slot[pl.ds(lax.rem(head, 8), 128, stride=8), :]
            mid_ref[j * 128 : (j + 1) * 128, a * HD : (a + 1) * HD] = mid.astype(BF)
            far.append(slot[pl.ds(head, 8, stride=128), :])
    for a in range(3):
        both = jnp.concatenate([far[a], far[3 + a]], 0)
        far_ref[:, a * HD : (a + 1) * HD] = both.astype(BF)


def near_forward_kernel(q_ref, k_ref, v_ref, o_ref, lse_ref):
    for c in range(2):
        rows = slice(c * 256, (c + 1) * 256)
        n = (c + 1) * 256
        s = dot_nt(q_ref[rows, :], k_ref[:n, :]) * SCALE
        keep = iota((256, n), 1) <= iota((256, n), 0) + c * 256
        s = jnp.where(keep, s, NEG)
        top = jnp.max(s, axis=1, keepdims=True)
        p = jnp.exp(s - top)
        total = jnp.sum(p, axis=1, keepdims=True)
        o = dot_nn(p.astype(BF), v_ref[:n, :])
        o_ref[0, rows, :] = o / total
        lse_ref[0, rows, :] = jnp.broadcast_to(top + jnp.log(total), (256, HD))


def mid_slots(s, shape, axis):
    n = iota(shape, axis)
    pos = n // 128
    other = s ^ ((pos & 1) * 2 + (pos >> 1))
    return (other & 3) * 128 + (n & 127)


def mid_forward_kernel(idx, mid_ref, o_ref, lse_ref):
    s_idx = idx[0]
    key_slot = mid_slots(s_idx, (128, SEG), 1)
    query_slot = (s_idx & 3) * 128 + iota((128, SEG), 0)
    keep = key_slot <= query_slot
    for j in range(2):
        q = mid_ref[j * 128 : (j + 1) * 128, 2 * HD :]
        k = jnp.concatenate(
            [mid_ref[p * 256 + j * 128 : p * 256 + (j + 1) * 128, :HD] for p in range(4)], 0
        )
        v = jnp.concatenate(
            [mid_ref[p * 256 + j * 128 : p * 256 + (j + 1) * 128, HD : 2 * HD] for p in range(4)], 0
        )
        s = jnp.where(keep, dot_nt(q, k) * SCALE, NEG)
        top = jnp.max(s, axis=1, keepdims=True)
        p = jnp.exp(s - top)
        total = jnp.sum(p, axis=1, keepdims=True)
        o = dot_nn(p.astype(BF), v)
        o_ref[j * 128 : (j + 1) * 128, :] = o / total
        lse_ref[j * 128 : (j + 1) * 128, :] = jnp.broadcast_to(top + jnp.log(total), (128, HD))


def far_places(s):
    n, row = iota((32, 1024), 1), iota((32, 1024), 0)
    pos = n // 32
    flips = (pos & 1) * 32 + (pos & 2) * 8 + (pos & 4) * 2 + ((pos & 8) >> 1) + ((pos & 16) >> 3)
    place = (((s | 1) ^ flips) - ((n >> 4) & 1)) * 8 + (n & 7)
    mine = ((s | 1) - (row >> 4)) * 8 + (row & 7)
    return ((n >> 3) & 1) == ((row >> 3) & 1), place, mine


def by_parity(idx, if_odd, if_even):
    odd = (iota(if_odd.shape, 0) * 0 + (idx[0] & 1)) == 1
    return jnp.where(odd, if_odd, if_even)


def far_keep_forward(s):
    same_head, place, mine = far_places(s)
    return same_head & (place <= mine)


def far_keep_backward(s):
    same_head, place, mine = far_places(s)
    return same_head & (place >= mine)


def pre_kernel(
    idx, o0, lse0, o1, lse1, mid_o, mid_lse, g_ref, att_ref, lse_ref, far_ref, out_scr
):
    for j in range(2):
        head = idx[1] * 2 + j
        picked = pl.ds(lax.rem(head, 8), 128, stride=8)
        distant = pl.ds(head, 8, stride=128)
        own = slice(j * 128, (j + 1) * 128)
        so, sl = out_scr.at[j], lse_ref.at[j]
        so[:SEG, :], so[SEG:, :] = o0[j], o1[j]
        sl[:SEG, :], sl[SEG:, :] = lse0[j], lse1[j]
        l1, l2 = sl[picked, :], mid_lse[own, :]
        peak = jnp.maximum(l1, l2)
        e1, e2 = jnp.exp(l1 - peak), jnp.exp(l2 - peak)
        den = e1 + e2
        so[picked, :] = (e1 * so[picked, :] + e2 * mid_o[own, :]) / den
        sl[picked, :] = peak + jnp.log(den)
        far_ref[j * 8 : (j + 1) * 8, :] = so[distant, :]
        far_ref[16 + j * 8 : 24 + j * 8, :] = sl[distant, :]
    lane = iota((128, HD), 1)
    row = iota((128, HD), 0)
    for b in range(8):
        rows = slice(b * 128, (b + 1) * 128)
        at, g = [], []
        for j in range(2):
            a16 = out_scr[j, rows, :].astype(BF)
            att_ref[rows, j * HD : (j + 1) * HD] = a16
            at.append(jnp.where(row == idx[1] * 2 + j, 0.0, a16.astype(F32)))
            g.append(g_ref[rows, j * HD : (j + 1) * HD].astype(F32))
            out_scr[j, rows, :] = g[j]
        sums = (
            at[0] + at[1],
            at[0] * at[0] + at[1] * at[1],
            g[0] * at[0] + g[1] * at[1],
            g[0] + g[1],
        )
        block = jnp.zeros((128, HD), F32)
        for i, term in enumerate(sums):
            block = jnp.where(lane == i, jnp.sum(term, axis=1, keepdims=True), block)
        far_ref[48 + b * 4 : 52 + b * 4, :] = block.T[:4, :]
    for j in range(2):
        distant = pl.ds(idx[1] * 2 + j, 8, stride=128)
        far_ref[32 + j * 8 : 40 + j * 8, :] = out_scr.at[j][distant, :]


def norm_terms(total, squares, cross, g_total):
    mean = total / D
    rstd = lax.rsqrt(squares / D - mean * mean + EPS)
    return mean, rstd, g_total / D, rstd * (cross - mean * g_total) / D


def stat_pack(lse, delta, lane):
    pack = jnp.zeros(lane.shape, F32)
    for i, term in enumerate(split3(lse) + split3(delta)):
        pack = jnp.where(lane == i, term, pack)
    return pack


def far_kernel(idx, far_all, own_ref, mate_ref, packs_ref, fix_ref, col_scr):
    q = far_all[:32, 2 * HD :]
    s = jnp.where(far_keep_forward(idx[0]), dot_nt(q, far_all[:, :HD]) * SCALE, NEG)
    top = jnp.max(s, axis=1, keepdims=True)
    p = jnp.exp(s - top)
    total = jnp.sum(p, axis=1, keepdims=True)
    o3 = dot_nn(p.astype(BF), far_all[:, HD : 2 * HD]) / total
    l3 = top + jnp.log(total)
    o12 = jnp.concatenate([own_ref[:16], mate_ref[:16]], 0)
    l12 = jnp.concatenate([own_ref[16:32], mate_ref[16:32]], 0)
    g = jnp.concatenate([own_ref[32:48], mate_ref[32:48]], 0)
    peak = jnp.maximum(l12, l3)
    e12, e3 = jnp.exp(l12 - peak), jnp.exp(l3 - peak)
    den = e12 + e3
    at16 = ((e12 * o12 + e3 * o3) / den).astype(BF)
    at = at16.astype(F32)
    lse = peak + jnp.log(den)

    others = [[], [], [], []]
    lane64 = iota((64, HD), 1)
    for half in range(2):
        for j in range(2):
            cs = col_scr.at[half * 2 + j]
            chosen = jnp.where(lane64 == idx[1] * 2 + j, mate_ref[48:], 0.0)
            cs[...] = jnp.broadcast_to(jnp.sum(chosen, axis=1, keepdims=True), (64, HD))
            for k in range(4):
                others[k].append(cs[pl.ds(half * 32 + k, 8, stride=4), :])
    others = [jnp.concatenate(part, 0) for part in others]
    lane, row = iota((32, HD), 1), iota((32, HD), 0)
    here = lane == (row & 7) * 16 + idx[1] * 2 + ((row >> 3) & 1)
    sums = []
    fix_ref[...] = jnp.zeros((8, HD), F32)
    for k, term in enumerate((at, at * at, g * at)):
        mine = jnp.sum(term, axis=1, keepdims=True)
        sums.append(others[k] + mine)
        placed = jnp.where(here, mine, 0.0)
        for half in range(2):
            own = placed[half * 16 : half * 16 + 16]
            fix_ref[half * 4 + k : half * 4 + k + 1, :] = jnp.sum(own, axis=0, keepdims=True)
    mean, rstd, sg, sgx = norm_terms(sums[0], sums[1], sums[2], others[3])
    x = (at - mean) * rstd
    grad = (rstd * (g - sg - x * sgx)).astype(BF)
    delta = jnp.sum(grad.astype(F32) * at, axis=1, keepdims=True)
    packs_ref[:32, :HD] = grad
    delta = jnp.broadcast_to(delta, (32, HD))
    packs_ref[:32, HD:] = stat_pack(lse, delta, lane).astype(BF)
    packs_ref[32:, :HD] = at16
    packs_ref[32:, HD:] = at16


def stat_cols(pack):
    pack = pack.astype(F32)
    lse = pack[:, 0:1] + pack[:, 1:2] + pack[:, 2:3]
    delta = pack[:, 3:4] + pack[:, 4:5] + pack[:, 5:6]
    return lse, delta


def far_query_kernel(idx, far_all, packs, dq_ref):
    @pl.when((idx[0] & 1) == 0)
    def _():
        k_all, v_all = far_all[:, :HD], far_all[:, HD : 2 * HD]
        lse, delta = stat_cols(packs[:32, HD:])
        keep = far_keep_forward(idx[0])
        s = jnp.where(keep, dot_nt(far_all[:32, 2 * HD :], k_all) * SCALE, NEG)
        p = jnp.exp(s - lse)
        ds = (p * (dot_nt(packs[:32, :HD], v_all) - delta)).astype(BF)
        dq_ref[...] = dot_nn(ds, k_all) * SCALE


def norm_kernel(
    idx,
    mate_ref,
    stat_ref,
    fix_own,
    fix_got,
    packs_own,
    packs_got,
    att_ref,
    g_ref,
    lse_in,
    normed_ref,
    grad_ref,
    delta_ref,
    lse_ref,
    mid_ref,
    att_scr,
    sum_scr,
):
    sums = by_parity(idx, mate_ref[48:80], stat_ref[32:])
    fixes = by_parity(idx, fix_own[:4], fix_got[4:])
    far_at = by_parity(
        idx, packs_own[32:48, :HD].astype(F32), packs_got[48:, :HD].astype(F32)
    )
    far_stat = by_parity(
        idx, packs_own[:16, HD:].astype(F32), packs_got[16:32, HD:].astype(F32)
    )
    far_lse = jnp.broadcast_to(stat_cols(far_stat)[0], (16, HD))
    for j in range(2):
        distant = pl.ds(idx[1] * 2 + j, 8, stride=128)
        at, lse = att_scr.at[j], lse_ref.at[j]
        at[...] = att_ref[:, j * HD : (j + 1) * HD].astype(F32)
        at[distant, :] = far_at[j * 8 : j * 8 + 8]
        lse[...] = lse_in[j]
        lse[distant, :] = far_lse[j * 8 : j * 8 + 8]
    for b in range(8):
        fix = jnp.concatenate(
            [fixes[:, b * 16 : (b + 1) * 16], jnp.zeros((4, HD - 16), F32)], 1
        )
        sum_scr[b * 4 : b * 4 + 4, :] = sums[b * 4 : b * 4 + 4] + fix
    terms = norm_terms(*(sum_scr[pl.ds(k, 8, stride=4), :] for k in range(4)))
    cols = jnp.concatenate(list(terms) + [jnp.zeros((96, HD), F32)], 0).T
    for b in range(8):
        rows = slice(b * 128, (b + 1) * 128)
        mean, rstd, sg, sgx = (cols[:, i * 8 + b : i * 8 + b + 1] for i in range(4))
        for j in range(2):
            at = att_scr[j, rows, :]
            x = (at - mean) * rstd
            normed_ref[rows, j * HD : (j + 1) * HD] = x.astype(BF)
            g = g_ref[rows, j * HD : (j + 1) * HD].astype(F32)
            grad = (rstd * (g - sg - x * sgx)).astype(BF)
            grad_ref[rows, j * HD : (j + 1) * HD] = grad
            grad = grad.astype(F32)
            delta = jnp.sum(grad * at, axis=1, keepdims=True)
            delta_ref[j, rows, :] = jnp.broadcast_to(delta, (128, HD))
            att_scr[j, rows, :] = grad
    lane = iota((128, HD), 1)
    for j in range(2):
        picked = pl.ds(lax.rem(idx[1] * 2 + j, 8), 128, stride=8)
        own = slice(j * 128, (j + 1) * 128)
        mid_ref[own, :HD] = att_scr.at[j][picked, :].astype(BF)
        pack = stat_pack(lse_ref.at[j][picked, :], delta_ref.at[j][picked, :], lane)
        mid_ref[own, HD:] = pack.astype(BF)


def near_backward_kernel(
    q_ref, k_ref, v_ref, g_ref, lse_ref, delta_ref, dq_ref, dk_ref, dv_ref
):
    for c in range(2):
        keys = slice(c * 256, (c + 1) * 256)
        rows = slice(c * 256, 512)
        n = 512 - c * 256
        q, g = q_ref[rows, :], g_ref[rows, :]
        k, v = k_ref[keys, :], v_ref[keys, :]
        lse = jnp.concatenate([lse_ref[0, rows, :]] * 2, 1)
        delta = jnp.concatenate([delta_ref[0, rows, :]] * 2, 1)
        s = dot_nt(q, k) * SCALE
        keep = iota((n, 256), 1) <= iota((n, 256), 0)
        p = jnp.exp(jnp.where(keep, s, NEG) - lse)
        ds = (p * (dot_nt(g, v) - delta)).astype(BF)
        p = p.astype(BF)
        dv_ref[0, keys, :] = dot_tn(p, g)
        dk_ref[0, keys, :] = dot_tn(ds, q) * SCALE
        dq = dot_nn(ds, k) * SCALE
        if c == 0:
            dq_ref[0, :, :] = dq
        else:
            dq_ref[0, rows, :] += dq


def query_grad_kernel(idx, dq0, dq1, mid_ref, mid_g, dq_got, dq_own, out_ref, scr, far_scr):
    s_idx = idx[0]
    far_dq = by_parity(idx, dq_got[:16], dq_own[16:])
    key_slot = mid_slots(s_idx, (128, SEG), 1)
    query_slot = (s_idx & 3) * 128 + iota((128, SEG), 0)
    keep = key_slot <= query_slot
    for j in range(2):
        head = idx[1] * 2 + j
        own = slice(j * 128, (j + 1) * 128)
        q = mid_ref[own, 2 * HD :]
        g = mid_g[own, :HD]
        lse, delta = stat_cols(mid_g[own, HD:])
        k = jnp.concatenate(
            [mid_ref[p * 256 + j * 128 : p * 256 + (j + 1) * 128, :HD] for p in range(4)], 0
        )
        v = jnp.concatenate(
            [mid_ref[p * 256 + j * 128 : p * 256 + (j + 1) * 128, HD : 2 * HD] for p in range(4)], 0
        )
        s = jnp.where(keep, dot_nt(q, k) * SCALE, NEG)
        p = jnp.exp(s - lse)
        ds = (p * (dot_nt(g, v) - delta)).astype(BF)
        fs = far_scr.at[j]
        fs[...] = dot_nn(ds, k) * SCALE
        spread = pl.ds(head // 8, 8, stride=16)
        fs[spread, :] = fs[spread, :] + far_dq[j * 8 : (j + 1) * 8]
        picked = pl.ds(lax.rem(head, 8), 128, stride=8)
        sc = scr.at[j]
        sc[:SEG, :], sc[SEG:, :] = dq0[j], dq1[j]
        sc[picked, :] = sc[picked, :] + fs[...]
        out_ref[:, j * HD : (j + 1) * HD] = sc[...].astype(BF)


def stat_rows(packs):
    lane, row = iota((8, HD), 1), iota((8, HD), 0)
    pick = ((row == lane // 3) & (lane < 6)).astype(F32).astype(BF)
    stats = dot_nt(pick, packs)
    return stats[0:1], stats[1:2]


def far_key_kernel(idx, far_all, grads, out_ref):
    @pl.when((idx[0] & 1) == 0)
    def _():
        lse, delta = stat_rows(grads[:, HD:])
        k, v = far_all[:32, :HD], far_all[:32, HD : 2 * HD]
        q_all, g_all = far_all[:, 2 * HD :], grads[:, :HD]
        s = jnp.where(far_keep_backward(idx[0]), dot_nt(k, q_all) * SCALE, NEG)
        p = jnp.exp(s - lse)
        ds = (p * (dot_nt(v, g_all) - delta)).astype(BF)
        out_ref[:32, :] = dot_nn(ds, q_all) * SCALE
        out_ref[32:, :] = dot_nn(p.astype(BF), g_all)


def mid_key_kernel(idx, dk0, dk1, dv0, dv1, mid_ref, grads, dk_ref, dv_ref):
    s_idx = idx[0]
    all_lse, all_delta = stat_rows(grads[:, HD:])
    query_slot = mid_slots(s_idx, (128, SEG), 1)
    key_slot = (s_idx & 3) * 128 + iota((128, SEG), 0)
    keep = key_slot <= query_slot
    for j in range(2):
        own = slice(j * 128, (j + 1) * 128)
        places = [slice(p * 256 + j * 128, p * 256 + (j + 1) * 128) for p in range(4)]
        k, v = mid_ref[own, :HD], mid_ref[own, HD : 2 * HD]
        q = jnp.concatenate([mid_ref[r, 2 * HD :] for r in places], 0)
        g = jnp.concatenate([grads[r, :HD] for r in places], 0)
        lse = jnp.concatenate([all_lse[:, r] for r in places], 1)
        delta = jnp.concatenate([all_delta[:, r] for r in places], 1)
        s = jnp.where(keep, dot_nt(k, q) * SCALE, NEG)
        p = jnp.exp(s - lse)
        ds = (p * (dot_nt(v, g) - delta)).astype(BF)
        picked = pl.ds(lax.rem(idx[1] * 2 + j, 8), 128, stride=8)
        for near0, near1, mid, out_ref in (
            (dk0, dk1, dot_nn(ds, q) * SCALE, dk_ref),
            (dv0, dv1, dot_nn(p.astype(BF), g), dv_ref),
        ):
            out = out_ref.at[j]
            out[:SEG, :], out[SEG:, :] = near0[j], near1[j]
            out[picked, :] = out[picked, :] + mid


def key_grad_kernel(idx, dk_in, dv_in, far_got, far_own, dk_out, dv_out, whole_ref, scr):
    for j in range(2):
        distant = pl.ds(idx[1] * 2 + j, 8, stride=128)
        for a, (near, out) in enumerate(((dk_in, dk_out), (dv_in, dv_out))):
            row = a * 32 + j * 8
            far = by_parity(idx, far_got[row : row + 8], far_own[row + 16 : row + 24])
            whole_ref[a, :, j * HD : (j + 1) * HD] = far
            sc = scr.at[j * 2 + a]
            sc[...] = near[j]
            sc[distant, :] = sc[distant, :] + far
            out[:, j * HD : (j + 1) * HD] = sc[...].astype(BF)


def exchange(x, bit):
    return lax.ppermute(x, "seq", [(i, i ^ bit) for i in range(64)])


def chip_exchange(x, bit, parity):
    return lax.ppermute(x, "seq", [(i, i ^ bit) for i in range(parity, 64, 2)])


def head_exchange(x, bit, parity):
    pairs = [(s * 8 + h, s * 8 + (h ^ bit)) for s in range(parity, 64, 2) for h in range(8)]
    return lax.ppermute(x, ("seq", "head"), pairs)


def to_odd(x):
    return lax.ppermute(x, "seq", [(i, i + 1) for i in range(0, 64, 2)])


def to_even(x):
    return lax.ppermute(x, "seq", [(i + 1, i) for i in range(0, 64, 2)])


def joined(a, b):
    return jnp.concatenate([a, b], 0)


def after(arrays):
    return lax.optimization_barrier(arrays)


def sds(shape, dtype):
    return jax.ShapeDtypeStruct(shape, dtype)


def local(queries, keys, values, out_grad):
    seq_index = lax.axis_index("seq")
    head_index = lax.axis_index("head")
    idx = jnp.stack([seq_index, head_index]).astype(jnp.int32)

    mid0, far0 = pl.pallas_call(
        select_kernel,
        out_shape=(sds((256, 384), BF), sds((16, 384), BF)),
        in_specs=[SMEM, VMEM, VMEM, VMEM],
        out_specs=(VMEM, VMEM),
        scratch_shapes=[pltpu.VMEM((6, TOK, HD), F32)],
        compiler_params=PARAMS,
        cost_estimate=cost(10**6, 2 * 10**6),
        name="select",
    )(idx, queries, keys, values)

    unit = pl.BlockSpec((SEG, HD), lambda b, j: (b, j))
    by_head = pl.BlockSpec((1, SEG, HD), lambda b, j: (j, b, 0))
    by_head_shape = sds((2, TOK, HD), F32)
    half = pl.BlockSpec((1, SEG, HD), lambda j: (j, 0, 0))
    half_shape = sds((2, SEG, HD), F32)

    def near_forward(block):
        part = pl.BlockSpec((SEG, HD), lambda j: (block, j))
        return pl.pallas_call(
            near_forward_kernel,
            grid=(2,),
            out_shape=(half_shape, half_shape),
            in_specs=[part, part, part],
            out_specs=(half, half),
            compiler_params=PARAMS,
            cost_estimate=cost(4 * 10**8, 2 * 10**6, 10**6),
            name=f"near_forward_{block}",
        )(queries, keys, values)

    mid1 = exchange(mid0, 2)
    mate_far = to_odd(far0)
    near0, near1 = near_forward(0), near_forward(1)
    mid_two, far1, near0, near1 = after(
        (joined(mid0, mid1), joined(far0, mate_far), near0, near1)
    )
    mid2 = exchange(mid_two, 1)
    mid_all = joined(mid_two, mid2)
    mid_o, mid_lse = pl.pallas_call(
        mid_forward_kernel,
        out_shape=(sds((256, HD), F32), sds((256, HD), F32)),
        in_specs=[SMEM, VMEM],
        out_specs=(VMEM, VMEM),
        compiler_params=PARAMS,
        cost_estimate=cost(2 * 10**8, 10**6, 10**5),
        name="mid_forward",
    )(idx, mid_all)

    att, lse12, bundle = pl.pallas_call(
        pre_kernel,
        out_shape=(sds((TOK, 256), BF), by_head_shape, sds((80, HD), F32)),
        in_specs=[SMEM] + [VMEM] * 7,
        out_specs=(VMEM,) * 3,
        scratch_shapes=[pltpu.VMEM((2, TOK, HD), F32)],
        compiler_params=PARAMS,
        cost_estimate=cost(10**7, 4 * 10**6, 10**5),
        name="pre",
    )(idx, *near0, *near1, mid_o, mid_lse, out_grad)
    far1, bundle = after((far1, bundle))
    mate_stats = to_even(bundle[48:])
    from1 = chip_exchange(far1, 32, 1)
    stats = joined(mate_stats, bundle[48:])
    sums1 = head_exchange(stats, 2, 0)
    far2, stats = after((joined(far1, from1), stats + sums1))
    from2 = chip_exchange(far2, 16, 1)
    sums2 = head_exchange(stats, 1, 0)
    far4, stats = after((joined(far2, from2), stats + sums2))
    from4 = chip_exchange(far4, 8, 1)
    sums3 = head_exchange(stats, 4, 0)
    far8 = joined(far4, from4)
    from8 = chip_exchange(far8, 4, 1)
    far16 = joined(far8, from8)
    from16 = chip_exchange(far16, 2, 1)
    stats = stats + sums3
    mate = to_odd(joined(bundle[:48], stats))
    far_all = joined(far16, from16)
    far_all, mate = after((far_all, mate))
    far_even = to_even(far_all)

    packs, fix = pl.pallas_call(
        far_kernel,
        out_shape=(sds((64, 256), BF), sds((8, HD), F32)),
        in_specs=[SMEM] + [VMEM] * 3,
        out_specs=(VMEM,) * 2,
        scratch_shapes=[pltpu.VMEM((4, 64, HD), F32)],
        compiler_params=PARAMS,
        cost_estimate=cost(10**7, 10**6, 10**5),
        name="far",
    )(idx, far_all, bundle, mate)

    packs_even = to_even(packs)
    fix1 = head_exchange(fix, 2, 1)
    part0 = packs_even[:32]
    part1 = chip_exchange(part0, 32, 0)
    part_a, fix = after((joined(part0, part1), fix + fix1))
    fix2 = head_exchange(fix, 1, 1)
    part2 = chip_exchange(part_a, 16, 0)
    far_dq = pl.pallas_call(
        far_query_kernel,
        out_shape=sds((32, HD), F32),
        in_specs=[SMEM] + [VMEM] * 2,
        out_specs=VMEM,
        compiler_params=PARAMS,
        cost_estimate=cost(10**7, 10**6, 10**5),
        name="far_query",
    )(idx, far_even, packs_even)
    part_b, fix, far_dq = after((joined(part_a, part2), fix + fix2, far_dq))
    mate_dq = to_odd(far_dq)
    fix3 = head_exchange(fix, 4, 1)
    part3 = chip_exchange(part_b, 8, 0)
    part_c, fix = after((joined(part_b, part3), fix + fix3))
    part4 = chip_exchange(part_c, 4, 0)
    fix_even = to_even(fix)
    normed, grad, delta, lse, mid_g = pl.pallas_call(
        norm_kernel,
        out_shape=(
            sds((TOK, 256), BF),
            sds((TOK, 256), BF),
            by_head_shape,
            by_head_shape,
            sds((256, 256), BF),
        ),
        in_specs=[SMEM] + [VMEM] * 9,
        out_specs=(VMEM,) * 5,
        scratch_shapes=[pltpu.VMEM((2, TOK, HD), F32), pltpu.VMEM((32, HD), F32)],
        compiler_params=PARAMS,
        cost_estimate=cost(10**7, 4 * 10**6),
        name="norm",
    )(idx, mate, stats, fix, fix_even, packs, packs_even, att, out_grad, lse12)

    def near_backward(block):
        part = pl.BlockSpec((SEG, HD), lambda j: (block, j))
        stat = pl.BlockSpec((1, SEG, HD), lambda j: (j, block, 0))
        return pl.pallas_call(
            near_backward_kernel,
            grid=(2,),
            out_shape=(half_shape,) * 3,
            in_specs=[part] * 4 + [stat] * 2,
            out_specs=(half,) * 3,
            compiler_params=PARAMS,
            cost_estimate=cost(10**9, 4 * 10**6, 10**6),
            name=f"near_backward_{block}",
        )(queries, keys, values, grad, lse, delta)

    part_d, mid_g = after((joined(part_c, part4), mid_g))
    mid_g1 = exchange(mid_g, 2)
    part5 = chip_exchange(part_d, 2, 0)
    dq0, dk0, dv0 = near_backward(0)
    dq1, dk1, dv1 = near_backward(1)
    mid_gs, far_gs, dq0, dq1 = after(
        (joined(mid_g, mid_g1), joined(part_d, part5), dq0, dq1)
    )
    mid_g2 = exchange(mid_gs, 1)

    far_kv = pl.pallas_call(
        far_key_kernel,
        out_shape=sds((64, HD), F32),
        in_specs=[SMEM] + [VMEM] * 2,
        out_specs=VMEM,
        compiler_params=PARAMS,
        cost_estimate=cost(10**7, 10**6, 10**5),
        name="far_key",
    )(idx, far_even, far_gs)
    mate_kv = to_odd(far_kv)

    grad_queries = pl.pallas_call(
        query_grad_kernel,
        out_shape=sds((TOK, 256), BF),
        in_specs=[SMEM] + [VMEM] * 6,
        out_specs=VMEM,
        scratch_shapes=[pltpu.VMEM((2, TOK, HD), F32), pltpu.VMEM((2, 128, HD), F32)],
        compiler_params=PARAMS,
        cost_estimate=cost(2 * 10**8, 3 * 10**6, 10**5),
        name="query_grad",
    )(idx, dq0, dq1, mid_all, mid_g, mate_dq, far_dq)

    mid_gall, grad_queries = after((joined(mid_gs, mid_g2), grad_queries))
    dk, dv = pl.pallas_call(
        mid_key_kernel,
        out_shape=(by_head_shape, by_head_shape),
        in_specs=[SMEM] + [VMEM] * 6,
        out_specs=(VMEM,) * 2,
        compiler_params=PARAMS,
        cost_estimate=cost(2 * 10**8, 4 * 10**6, 10**5),
        name="mid_key",
    )(idx, dk0, dk1, dv0, dv1, mid_all, mid_gall)

    grad_keys, grad_values, whole = pl.pallas_call(
        key_grad_kernel,
        out_shape=(sds((TOK, 256), BF), sds((TOK, 256), BF), sds((2, 8, 256), F32)),
        in_specs=[SMEM] + [VMEM] * 4,
        out_specs=(VMEM,) * 3,
        scratch_shapes=[pltpu.VMEM((4, TOK, HD), F32)],
        compiler_params=PARAMS,
        cost_estimate=cost(10**6, 4 * 10**6),
        name="key_grad",
    )(idx, dk, dv, mate_kv, far_kv)

    return normed, grad_queries, grad_keys, grad_values, whole


def solution(mesh):
    spec = P("seq", "head")
    return jax.shard_map(
        local,
        mesh=mesh,
        in_specs=(spec,) * 4,
        out_specs=(spec,) * 4 + (P(None, "seq", "head"),),
        check_vma=False,
    )
```

```python
import jax
import jax.numpy as jnp
from jax import lax
from jax.experimental import pallas as pl
from jax.experimental.pallas import tpu as pltpu
from jax.sharding import PartitionSpec as P

H = 16
HD = 128
D = H * HD
TOK = 1024
SEG = 512
NEG = -1e30
EPS = 1e-05
SCALE = HD ** (-0.5)
BF = jnp.bfloat16
F32 = jnp.float32
VMEM = pl.BlockSpec(memory_space=pltpu.VMEM)
SMEM = pl.BlockSpec(memory_space=pltpu.SMEM)
PARAMS = pltpu.CompilerParams(vmem_limit_bytes=16 * 1024 * 1024)


def dot_nt(a, b):
    return lax.dot_general(a, b, (((1,), (1,)), ((), ())), preferred_element_type=F32)


def dot_nn(a, b):
    return lax.dot_general(a, b, (((1,), (0,)), ((), ())), preferred_element_type=F32)


def dot_tn(a, b):
    return lax.dot_general(a, b, (((0,), (0,)), ((), ())), preferred_element_type=F32)


def iota(shape, axis):
    return lax.broadcasted_iota(jnp.int32, shape, axis)


def cost(flops, bytes_accessed, transcendentals=0):
    return pl.CostEstimate(
        flops=flops, bytes_accessed=bytes_accessed, transcendentals=transcendentals
    )


def split3(x):
    hi = x.astype(BF)
    rest = x - hi.astype(F32)
    mid = rest.astype(BF)
    low = (rest - mid.astype(F32)).astype(BF)
    return hi.astype(F32), mid.astype(F32), low.astype(F32)


def select_kernel(idx, q_ref, k_ref, v_ref, mid_ref, far_ref, wide):
    far = []
    for j in range(2):
        head = idx[1] * 2 + j
        for a, ref in enumerate((k_ref, v_ref, q_ref)):
            slot = wide.at[j * 3 + a]
            slot[...] = ref[:, j * HD : (j + 1) * HD].astype(F32)
            mid = slot[pl.ds(lax.rem(head, 8), 128, stride=8), :]
            mid_ref[j * 128 : (j + 1) * 128, a * HD : (a + 1) * HD] = mid.astype(BF)
            far.append(slot[pl.ds(head, 8, stride=128), :])
    for a in range(3):
        both = jnp.concatenate([far[a], far[3 + a]], 0)
        far_ref[:, a * HD : (a + 1) * HD] = both.astype(BF)


def near_forward_kernel(q_ref, k_ref, v_ref, o_ref, lse_ref):
    for c in range(2):
        rows = slice(c * 256, (c + 1) * 256)
        n = (c + 1) * 256
        s = dot_nt(q_ref[rows, :], k_ref[:n, :]) * SCALE
        keep = iota((256, n), 1) <= iota((256, n), 0) + c * 256
        s = jnp.where(keep, s, NEG)
        top = jnp.max(s, axis=1, keepdims=True)
        p = jnp.exp(s - top)
        total = jnp.sum(p, axis=1, keepdims=True)
        o = dot_nn(p.astype(BF), v_ref[:n, :])
        o_ref[0, rows, :] = o / total
        lse_ref[0, rows, :] = jnp.broadcast_to(top + jnp.log(total), (256, HD))


def mid_slots(s, shape, axis):
    n = iota(shape, axis)
    pos = n // 128
    other = s ^ ((pos & 1) * 2 + (pos >> 1))
    return (other & 3) * 128 + (n & 127)


def mid_forward_kernel(idx, mid_ref, o_ref, lse_ref):
    s_idx = idx[0]
    key_slot = mid_slots(s_idx, (128, SEG), 1)
    query_slot = (s_idx & 3) * 128 + iota((128, SEG), 0)
    keep = key_slot <= query_slot
    for j in range(2):
        q = mid_ref[j * 128 : (j + 1) * 128, 2 * HD :]
        k = jnp.concatenate(
            [mid_ref[p * 256 + j * 128 : p * 256 + (j + 1) * 128, :HD] for p in range(4)], 0
        )
        v = jnp.concatenate(
            [mid_ref[p * 256 + j * 128 : p * 256 + (j + 1) * 128, HD : 2 * HD] for p in range(4)], 0
        )
        s = jnp.where(keep, dot_nt(q, k) * SCALE, NEG)
        top = jnp.max(s, axis=1, keepdims=True)
        p = jnp.exp(s - top)
        total = jnp.sum(p, axis=1, keepdims=True)
        o = dot_nn(p.astype(BF), v)
        o_ref[j * 128 : (j + 1) * 128, :] = o / total
        lse_ref[j * 128 : (j + 1) * 128, :] = jnp.broadcast_to(top + jnp.log(total), (128, HD))


def far_places(s):
    n, row = iota((32, 1024), 1), iota((32, 1024), 0)
    pos = n // 32
    flips = (pos & 1) * 32 + (pos & 2) * 8 + (pos & 4) * 2 + ((pos & 8) >> 1) + ((pos & 16) >> 3)
    place = (((s | 1) ^ flips) - ((n >> 4) & 1)) * 8 + (n & 7)
    mine = ((s | 1) - (row >> 4)) * 8 + (row & 7)
    return ((n >> 3) & 1) == ((row >> 3) & 1), place, mine


def by_parity(idx, if_odd, if_even):
    odd = (iota(if_odd.shape, 0) * 0 + (idx[0] & 1)) == 1
    return jnp.where(odd, if_odd, if_even)


def far_keep_forward(s):
    same_head, place, mine = far_places(s)
    return same_head & (place <= mine)


def far_keep_backward(s):
    same_head, place, mine = far_places(s)
    return same_head & (place >= mine)


def pre_kernel(
    idx, o0, lse0, o1, lse1, mid_o, mid_lse, g_ref, att_ref, lse_ref, far_ref, out_scr
):
    for j in range(2):
        head = idx[1] * 2 + j
        picked = pl.ds(lax.rem(head, 8), 128, stride=8)
        distant = pl.ds(head, 8, stride=128)
        own = slice(j * 128, (j + 1) * 128)
        so, sl = out_scr.at[j], lse_ref.at[j]
        so[:SEG, :], so[SEG:, :] = o0[j], o1[j]
        sl[:SEG, :], sl[SEG:, :] = lse0[j], lse1[j]
        l1, l2 = sl[picked, :], mid_lse[own, :]
        peak = jnp.maximum(l1, l2)
        e1, e2 = jnp.exp(l1 - peak), jnp.exp(l2 - peak)
        den = e1 + e2
        so[picked, :] = (e1 * so[picked, :] + e2 * mid_o[own, :]) / den
        sl[picked, :] = peak + jnp.log(den)
        far_ref[j * 8 : (j + 1) * 8, :] = so[distant, :]
        far_ref[16 + j * 8 : 24 + j * 8, :] = sl[distant, :]
    lane = iota((128, HD), 1)
    row = iota((128, HD), 0)
    table = jnp.zeros((128, HD), F32)
    for b in range(8):
        rows = slice(b * 128, (b + 1) * 128)
        at, g = [], []
        for j in range(2):
            a16 = out_scr[j, rows, :].astype(BF)
            att_ref[rows, j * HD : (j + 1) * HD] = a16
            at.append(jnp.where(row == idx[1] * 2 + j, 0.0, a16.astype(F32)))
            g.append(g_ref[rows, j * HD : (j + 1) * HD].astype(F32))
            out_scr[j, rows, :] = g[j]
        sums = (
            at[0] + at[1],
            at[0] * at[0] + at[1] * at[1],
            g[0] * at[0] + g[1] * at[1],
            g[0] + g[1],
        )
        for i, term in enumerate(sums):
            table = jnp.where(lane == b * 4 + i, jnp.sum(term, axis=1, keepdims=True), table)
    far_ref[48:, :] = table.T[:32, :]
    for j in range(2):
        distant = pl.ds(idx[1] * 2 + j, 8, stride=128)
        far_ref[32 + j * 8 : 40 + j * 8, :] = out_scr.at[j][distant, :]


def norm_terms(total, squares, cross, g_total):
    mean = total / D
    rstd = lax.rsqrt(squares / D - mean * mean + EPS)
    return mean, rstd, g_total / D, rstd * (cross - mean * g_total) / D


def stat_pack(lse, delta, lane):
    pack = jnp.zeros(lane.shape, F32)
    for i, term in enumerate(split3(lse) + split3(delta)):
        pack = jnp.where(lane == i, term, pack)
    return pack


def far_kernel(idx, far_all, rows_ref, own_ref, mate_ref, packs_ref, fix_ref, col_scr):
    q = rows_ref[:, 2 * HD :]
    s = jnp.where(far_keep_forward(idx[0]), dot_nt(q, far_all[:, :HD]) * SCALE, NEG)
    top = jnp.max(s, axis=1, keepdims=True)
    p = jnp.exp(s - top)
    total = jnp.sum(p, axis=1, keepdims=True)
    o3 = dot_nn(p.astype(BF), far_all[:, HD : 2 * HD]) / total
    l3 = top + jnp.log(total)
    o12 = jnp.concatenate([own_ref[:16], mate_ref[:16]], 0)
    l12 = jnp.concatenate([own_ref[16:32], mate_ref[16:32]], 0)
    g = jnp.concatenate([own_ref[32:48], mate_ref[32:48]], 0)
    peak = jnp.maximum(l12, l3)
    e12, e3 = jnp.exp(l12 - peak), jnp.exp(l3 - peak)
    den = e12 + e3
    at16 = ((e12 * o12 + e3 * o3) / den).astype(BF)
    at = at16.astype(F32)
    lse = peak + jnp.log(den)

    others = [[], [], [], []]
    lane64 = iota((64, HD), 1)
    for half in range(2):
        for j in range(2):
            cs = col_scr.at[half * 2 + j]
            chosen = jnp.where(lane64 == idx[1] * 2 + j, mate_ref[48:], 0.0)
            cs[...] = jnp.broadcast_to(jnp.sum(chosen, axis=1, keepdims=True), (64, HD))
            for k in range(4):
                others[k].append(cs[pl.ds(half * 32 + k, 8, stride=4), :])
    others = [jnp.concatenate(part, 0) for part in others]
    lane, row = iota((32, HD), 1), iota((32, HD), 0)
    here = lane == (row & 7) * 16 + idx[1] * 2 + ((row >> 3) & 1)
    sums = []
    fix_ref[...] = jnp.zeros((8, HD), F32)
    for k, term in enumerate((at, at * at, g * at)):
        mine = jnp.sum(term, axis=1, keepdims=True)
        sums.append(others[k] + mine)
        placed = jnp.where(here, mine, 0.0)
        for half in range(2):
            own = placed[half * 16 : half * 16 + 16]
            fix_ref[half * 4 + k : half * 4 + k + 1, :] = jnp.sum(own, axis=0, keepdims=True)
    mean, rstd, sg, sgx = norm_terms(sums[0], sums[1], sums[2], others[3])
    x = (at - mean) * rstd
    grad = (rstd * (g - sg - x * sgx)).astype(BF)
    delta = jnp.sum(grad.astype(F32) * at, axis=1, keepdims=True)
    packs_ref[:32, :HD] = grad
    delta = jnp.broadcast_to(delta, (32, HD))
    packs_ref[:32, HD : 2 * HD] = stat_pack(lse, delta, lane).astype(BF)
    packs_ref[:32, 2 * HD :] = q
    packs_ref[32:, :HD] = at16
    packs_ref[32:, HD : 2 * HD] = at16
    packs_ref[32:, 2 * HD :] = at16


def stat_cols(pack):
    pack = pack.astype(F32)
    lse = pack[:, 0:1] + pack[:, 1:2] + pack[:, 2:3]
    delta = pack[:, 3:4] + pack[:, 4:5] + pack[:, 5:6]
    return lse, delta


def far_query_kernel(idx, far_all, packs, dq_ref):
    @pl.when((idx[0] & 1) == 0)
    def _():
        k_all, v_all = far_all[:, :HD], far_all[:, HD : 2 * HD]
        lse, delta = stat_cols(packs[:32, HD : 2 * HD])
        keep = far_keep_forward(idx[0])
        s = jnp.where(keep, dot_nt(packs[:32, 2 * HD :], k_all) * SCALE, NEG)
        p = jnp.exp(s - lse)
        ds = (p * (dot_nt(packs[:32, :HD], v_all) - delta)).astype(BF)
        dq_ref[...] = dot_nn(ds, k_all) * SCALE


def norm_kernel(
    idx,
    mate_ref,
    stat_ref,
    fix_own,
    fix_got,
    packs_own,
    packs_got,
    att_ref,
    g_ref,
    lse_in,
    normed_ref,
    grad_ref,
    delta_ref,
    lse_ref,
    mid_ref,
    att_scr,
    sum_scr,
):
    sums = by_parity(idx, mate_ref[48:80], stat_ref[32:])
    fixes = by_parity(idx, fix_own[:4], fix_got[4:])
    far_at = by_parity(
        idx, packs_own[32:48, :HD].astype(F32), packs_got[48:, :HD].astype(F32)
    )
    far_stat = by_parity(
        idx,
        packs_own[:16, HD : 2 * HD].astype(F32),
        packs_got[16:32, HD : 2 * HD].astype(F32),
    )
    far_lse = jnp.broadcast_to(stat_cols(far_stat)[0], (16, HD))
    for j in range(2):
        distant = pl.ds(idx[1] * 2 + j, 8, stride=128)
        at, lse = att_scr.at[j], lse_ref.at[j]
        at[...] = att_ref[:, j * HD : (j + 1) * HD].astype(F32)
        at[distant, :] = far_at[j * 8 : j * 8 + 8]
        lse[...] = lse_in[j]
        lse[distant, :] = far_lse[j * 8 : j * 8 + 8]
    for b in range(8):
        fix = jnp.concatenate(
            [fixes[:, b * 16 : (b + 1) * 16], jnp.zeros((4, HD - 16), F32)], 1
        )
        sum_scr[b * 4 : b * 4 + 4, :] = sums[b * 4 : b * 4 + 4] + fix
    terms = norm_terms(*(sum_scr[pl.ds(k, 8, stride=4), :] for k in range(4)))
    cols = jnp.concatenate(list(terms) + [jnp.zeros((96, HD), F32)], 0).T
    for b in range(8):
        rows = slice(b * 128, (b + 1) * 128)
        mean, rstd, sg, sgx = (cols[:, i * 8 + b : i * 8 + b + 1] for i in range(4))
        for j in range(2):
            at = att_scr[j, rows, :]
            x = (at - mean) * rstd
            normed_ref[rows, j * HD : (j + 1) * HD] = x.astype(BF)
            g = g_ref[rows, j * HD : (j + 1) * HD].astype(F32)
            grad = (rstd * (g - sg - x * sgx)).astype(BF)
            grad_ref[rows, j * HD : (j + 1) * HD] = grad
            grad = grad.astype(F32)
            delta = jnp.sum(grad * at, axis=1, keepdims=True)
            delta_ref[j, rows, :] = jnp.broadcast_to(delta, (128, HD))
            att_scr[j, rows, :] = grad
    lane = iota((128, HD), 1)
    for j in range(2):
        picked = pl.ds(lax.rem(idx[1] * 2 + j, 8), 128, stride=8)
        own = slice(j * 128, (j + 1) * 128)
        mid_ref[own, :HD] = att_scr.at[j][picked, :].astype(BF)
        pack = stat_pack(lse_ref.at[j][picked, :], delta_ref.at[j][picked, :], lane)
        mid_ref[own, HD:] = pack.astype(BF)


def near_backward_kernel(
    q_ref, k_ref, v_ref, g_ref, lse_ref, delta_ref, dq_ref, dk_ref, dv_ref
):
    for c in range(2):
        keys = slice(c * 256, (c + 1) * 256)
        rows = slice(c * 256, 512)
        n = 512 - c * 256
        q, g = q_ref[rows, :], g_ref[rows, :]
        k, v = k_ref[keys, :], v_ref[keys, :]
        lse = jnp.concatenate([lse_ref[0, rows, :]] * 2, 1)
        delta = jnp.concatenate([delta_ref[0, rows, :]] * 2, 1)
        s = dot_nt(q, k) * SCALE
        keep = iota((n, 256), 1) <= iota((n, 256), 0)
        p = jnp.exp(jnp.where(keep, s, NEG) - lse)
        ds = (p * (dot_nt(g, v) - delta)).astype(BF)
        p = p.astype(BF)
        dv_ref[0, keys, :] = dot_tn(p, g)
        dk_ref[0, keys, :] = dot_tn(ds, q) * SCALE
        dq = dot_nn(ds, k) * SCALE
        if c == 0:
            dq_ref[0, :, :] = dq
        else:
            dq_ref[0, rows, :] += dq


def query_grad_kernel(idx, dq0, dq1, mid_ref, mid_g, far_got, far_own, out_ref, scr, far_scr):
    s_idx = idx[0]
    far_dq = by_parity(idx, far_got[64:80], far_own[80:])
    key_slot = mid_slots(s_idx, (128, SEG), 1)
    query_slot = (s_idx & 3) * 128 + iota((128, SEG), 0)
    keep = key_slot <= query_slot
    for j in range(2):
        head = idx[1] * 2 + j
        own = slice(j * 128, (j + 1) * 128)
        q = mid_ref[own, 2 * HD :]
        g = mid_g[own, :HD]
        lse, delta = stat_cols(mid_g[own, HD:])
        k = jnp.concatenate(
            [mid_ref[p * 256 + j * 128 : p * 256 + (j + 1) * 128, :HD] for p in range(4)], 0
        )
        v = jnp.concatenate(
            [mid_ref[p * 256 + j * 128 : p * 256 + (j + 1) * 128, HD : 2 * HD] for p in range(4)], 0
        )
        s = jnp.where(keep, dot_nt(q, k) * SCALE, NEG)
        p = jnp.exp(s - lse)
        ds = (p * (dot_nt(g, v) - delta)).astype(BF)
        fs = far_scr.at[j]
        fs[...] = dot_nn(ds, k) * SCALE
        spread = pl.ds(head // 8, 8, stride=16)
        fs[spread, :] = fs[spread, :] + far_dq[j * 8 : (j + 1) * 8]
        picked = pl.ds(lax.rem(head, 8), 128, stride=8)
        sc = scr.at[j]
        sc[:SEG, :], sc[SEG:, :] = dq0[j], dq1[j]
        sc[picked, :] = sc[picked, :] + fs[...]
        out_ref[:, j * HD : (j + 1) * HD] = sc[...].astype(BF)


def stat_rows(packs):
    lane, row = iota((8, HD), 1), iota((8, HD), 0)
    pick = ((row == lane // 3) & (lane < 6)).astype(F32).astype(BF)
    stats = dot_nt(pick, packs)
    return stats[0:1], stats[1:2]


def far_key_kernel(idx, far_all, grads, dq_ref, out_ref):
    @pl.when((idx[0] & 1) == 0)
    def _():
        lse, delta = stat_rows(grads[:, HD : 2 * HD])
        k, v = far_all[:32, :HD], far_all[:32, HD : 2 * HD]
        q_all, g_all = grads[:, 2 * HD :], grads[:, :HD]
        s = jnp.where(far_keep_backward(idx[0]), dot_nt(k, q_all) * SCALE, NEG)
        p = jnp.exp(s - lse)
        ds = (p * (dot_nt(v, g_all) - delta)).astype(BF)
        out_ref[:32, :] = dot_nn(ds, q_all) * SCALE
        out_ref[32:64, :] = dot_nn(p.astype(BF), g_all)
        out_ref[64:, :] = dq_ref[...]


def mid_key_kernel(idx, dk0, dk1, dv0, dv1, mid_ref, grads, dk_ref, dv_ref):
    s_idx = idx[0]
    all_lse, all_delta = stat_rows(grads[:, HD:])
    query_slot = mid_slots(s_idx, (128, SEG), 1)
    key_slot = (s_idx & 3) * 128 + iota((128, SEG), 0)
    keep = key_slot <= query_slot
    for j in range(2):
        own = slice(j * 128, (j + 1) * 128)
        places = [slice(p * 256 + j * 128, p * 256 + (j + 1) * 128) for p in range(4)]
        k, v = mid_ref[own, :HD], mid_ref[own, HD : 2 * HD]
        q = jnp.concatenate([mid_ref[r, 2 * HD :] for r in places], 0)
        g = jnp.concatenate([grads[r, :HD] for r in places], 0)
        lse = jnp.concatenate([all_lse[:, r] for r in places], 1)
        delta = jnp.concatenate([all_delta[:, r] for r in places], 1)
        s = jnp.where(keep, dot_nt(k, q) * SCALE, NEG)
        p = jnp.exp(s - lse)
        ds = (p * (dot_nt(v, g) - delta)).astype(BF)
        picked = pl.ds(lax.rem(idx[1] * 2 + j, 8), 128, stride=8)
        for near0, near1, mid, out_ref in (
            (dk0, dk1, dot_nn(ds, q) * SCALE, dk_ref),
            (dv0, dv1, dot_nn(p.astype(BF), g), dv_ref),
        ):
            out = out_ref.at[j]
            out[:SEG, :], out[SEG:, :] = near0[j], near1[j]
            out[picked, :] = out[picked, :] + mid


def key_grad_kernel(idx, dk_in, dv_in, far_got, far_own, dk_out, dv_out, whole_ref):
    row = iota((128, HD), 0)
    for j in range(2):
        here = row == idx[1] * 2 + j
        cols = slice(j * HD, (j + 1) * HD)
        for a, (near, out) in enumerate(((dk_in, dk_out), (dv_in, dv_out))):
            first = a * 32 + j * 8
            far = by_parity(idx, far_got[first : first + 8], far_own[first + 16 : first + 24])
            whole_ref[a, :, cols] = far
            for b in range(8):
                rows = slice(b * 128, (b + 1) * 128)
                total = near[j, rows, :] + jnp.where(here, far[b : b + 1], 0.0)
                out[rows, cols] = total.astype(BF)


def exchange(x, bit):
    return lax.ppermute(x, "seq", [(i, i ^ bit) for i in range(64)])


def chip_exchange(x, bit, parity):
    return lax.ppermute(x, "seq", [(i, i ^ bit) for i in range(parity, 64, 2)])


def head_exchange(x, bit, parity):
    pairs = [(s * 8 + h, s * 8 + (h ^ bit)) for s in range(parity, 64, 2) for h in range(8)]
    return lax.ppermute(x, ("seq", "head"), pairs)


def to_odd(x):
    return lax.ppermute(x, "seq", [(i, i + 1) for i in range(0, 64, 2)])


def to_even(x):
    return lax.ppermute(x, "seq", [(i + 1, i) for i in range(0, 64, 2)])


def joined(a, b):
    return jnp.concatenate([a, b], 0)


def after(arrays):
    return lax.optimization_barrier(arrays)


def sds(shape, dtype):
    return jax.ShapeDtypeStruct(shape, dtype)


def local(queries, keys, values, out_grad):
    seq_index = lax.axis_index("seq")
    head_index = lax.axis_index("head")
    idx = jnp.stack([seq_index, head_index]).astype(jnp.int32)

    mid0, far0 = pl.pallas_call(
        select_kernel,
        out_shape=(sds((256, 384), BF), sds((16, 384), BF)),
        in_specs=[SMEM, VMEM, VMEM, VMEM],
        out_specs=(VMEM, VMEM),
        scratch_shapes=[pltpu.VMEM((6, TOK, HD), F32)],
        compiler_params=PARAMS,
        cost_estimate=cost(10**6, 2 * 10**6),
        name="select",
    )(idx, queries, keys, values)

    unit = pl.BlockSpec((SEG, HD), lambda b, j: (b, j))
    by_head = pl.BlockSpec((1, SEG, HD), lambda b, j: (j, b, 0))
    by_head_shape = sds((2, TOK, HD), F32)
    half = pl.BlockSpec((1, SEG, HD), lambda j: (j, 0, 0))
    half_shape = sds((2, SEG, HD), F32)

    def near_forward(block):
        part = pl.BlockSpec((SEG, HD), lambda j: (block, j))
        return pl.pallas_call(
            near_forward_kernel,
            grid=(2,),
            out_shape=(half_shape, half_shape),
            in_specs=[part, part, part],
            out_specs=(half, half),
            compiler_params=PARAMS,
            cost_estimate=cost(4 * 10**8, 2 * 10**6, 10**6),
            name=f"near_forward_{block}",
        )(queries, keys, values)

    mid1 = exchange(mid0, 2)
    mate_far = to_odd(far0)
    near0, near1 = near_forward(0), near_forward(1)
    mid_two, far1, near0, near1 = after(
        (joined(mid0, mid1), joined(far0, mate_far), near0, near1)
    )
    mid2 = exchange(mid_two, 1)
    mid_all = joined(mid_two, mid2)
    mid_o, mid_lse = pl.pallas_call(
        mid_forward_kernel,
        out_shape=(sds((256, HD), F32), sds((256, HD), F32)),
        in_specs=[SMEM, VMEM],
        out_specs=(VMEM, VMEM),
        compiler_params=PARAMS,
        cost_estimate=cost(2 * 10**8, 10**6, 10**5),
        name="mid_forward",
    )(idx, mid_all)

    att, lse12, bundle = pl.pallas_call(
        pre_kernel,
        out_shape=(sds((TOK, 256), BF), by_head_shape, sds((80, HD), F32)),
        in_specs=[SMEM] + [VMEM] * 7,
        out_specs=(VMEM,) * 3,
        scratch_shapes=[pltpu.VMEM((2, TOK, HD), F32)],
        compiler_params=PARAMS,
        cost_estimate=cost(10**7, 4 * 10**6, 10**5),
        name="pre",
    )(idx, *near0, *near1, mid_o, mid_lse, out_grad)
    rows, bundle = after((far1, bundle))
    far1 = rows[:, : 2 * HD]
    mate_stats = to_even(bundle[48:])
    from1 = chip_exchange(far1, 32, 1)
    stats = joined(mate_stats, bundle[48:])
    sums1 = head_exchange(stats, 2, 0)
    far2, stats = after((joined(far1, from1), stats + sums1))
    from2 = chip_exchange(far2, 16, 1)
    sums2 = head_exchange(stats, 1, 0)
    far4, stats = after((joined(far2, from2), stats + sums2))
    from4 = chip_exchange(far4, 8, 1)
    sums3 = head_exchange(stats, 4, 0)
    far8 = joined(far4, from4)
    from8 = chip_exchange(far8, 4, 1)
    far16 = joined(far8, from8)
    from16 = chip_exchange(far16, 2, 1)
    stats = stats + sums3
    mate = to_odd(joined(bundle[:48], stats))
    far_all = joined(far16, from16)
    far_all, mate = after((far_all, mate))
    far_even = to_even(far_all)

    packs, fix = pl.pallas_call(
        far_kernel,
        out_shape=(sds((64, 384), BF), sds((8, HD), F32)),
        in_specs=[SMEM] + [VMEM] * 4,
        out_specs=(VMEM,) * 2,
        scratch_shapes=[pltpu.VMEM((4, 64, HD), F32)],
        compiler_params=PARAMS,
        cost_estimate=cost(10**7, 10**6, 10**5),
        name="far",
    )(idx, far_all, rows, bundle, mate)

    packs_even = to_even(packs)
    fix1 = head_exchange(fix, 2, 1)
    part0 = packs_even[:32]
    part1 = chip_exchange(part0, 32, 0)
    part_a, fix = after((joined(part0, part1), fix + fix1))
    fix2 = head_exchange(fix, 1, 1)
    part2 = chip_exchange(part_a, 16, 0)
    far_dq = pl.pallas_call(
        far_query_kernel,
        out_shape=sds((32, HD), F32),
        in_specs=[SMEM] + [VMEM] * 2,
        out_specs=VMEM,
        compiler_params=PARAMS,
        cost_estimate=cost(10**7, 10**6, 10**5),
        name="far_query",
    )(idx, far_even, packs_even)
    part_b, fix, far_dq = after((joined(part_a, part2), fix + fix2, far_dq))
    fix3 = head_exchange(fix, 4, 1)
    part3 = chip_exchange(part_b, 8, 0)
    part_c, fix = after((joined(part_b, part3), fix + fix3))
    part4 = chip_exchange(part_c, 4, 0)
    fix_even = to_even(fix)
    normed, grad, delta, lse, mid_g = pl.pallas_call(
        norm_kernel,
        out_shape=(
            sds((TOK, 256), BF),
            sds((TOK, 256), BF),
            by_head_shape,
            by_head_shape,
            sds((256, 256), BF),
        ),
        in_specs=[SMEM] + [VMEM] * 9,
        out_specs=(VMEM,) * 5,
        scratch_shapes=[pltpu.VMEM((2, TOK, HD), F32), pltpu.VMEM((32, HD), F32)],
        compiler_params=PARAMS,
        cost_estimate=cost(10**7, 4 * 10**6),
        name="norm",
    )(idx, mate, stats, fix, fix_even, packs, packs_even, att, out_grad, lse12)

    def near_backward(block):
        part = pl.BlockSpec((SEG, HD), lambda j: (block, j))
        stat = pl.BlockSpec((1, SEG, HD), lambda j: (j, block, 0))
        return pl.pallas_call(
            near_backward_kernel,
            grid=(2,),
            out_shape=(half_shape,) * 3,
            in_specs=[part] * 4 + [stat] * 2,
            out_specs=(half,) * 3,
            compiler_params=PARAMS,
            cost_estimate=cost(10**9, 4 * 10**6, 10**6),
            name=f"near_backward_{block}",
        )(queries, keys, values, grad, lse, delta)

    part_d, mid_g = after((joined(part_c, part4), mid_g))
    mid_g1 = exchange(mid_g, 2)
    part5 = chip_exchange(part_d, 2, 0)
    dq0, dk0, dv0 = near_backward(0)
    dq1, dk1, dv1 = near_backward(1)
    mid_gs, far_gs, dq0, dq1 = after(
        (joined(mid_g, mid_g1), joined(part_d, part5), dq0, dq1)
    )
    mid_g2 = exchange(mid_gs, 1)

    far_kv = pl.pallas_call(
        far_key_kernel,
        out_shape=sds((96, HD), F32),
        in_specs=[SMEM] + [VMEM] * 3,
        out_specs=VMEM,
        compiler_params=PARAMS,
        cost_estimate=cost(10**7, 10**6, 10**5),
        name="far_key",
    )(idx, far_even, far_gs, far_dq)
    mate_kv = to_odd(far_kv)

    mid_gall = joined(mid_gs, mid_g2)
    dk, dv = pl.pallas_call(
        mid_key_kernel,
        out_shape=(by_head_shape, by_head_shape),
        in_specs=[SMEM] + [VMEM] * 6,
        out_specs=(VMEM,) * 2,
        compiler_params=PARAMS,
        cost_estimate=cost(2 * 10**8, 4 * 10**6, 10**5),
        name="mid_key",
    )(idx, dk0, dk1, dv0, dv1, mid_all, mid_gall)

    mate_kv, dk = after((mate_kv, dk))

    grad_queries = pl.pallas_call(
        query_grad_kernel,
        out_shape=sds((TOK, 256), BF),
        in_specs=[SMEM] + [VMEM] * 6,
        out_specs=VMEM,
        scratch_shapes=[pltpu.VMEM((2, TOK, HD), F32), pltpu.VMEM((2, 128, HD), F32)],
        compiler_params=PARAMS,
        cost_estimate=cost(2 * 10**8, 3 * 10**6, 10**5),
        name="query_grad",
    )(idx, dq0, dq1, mid_all, mid_g, mate_kv, far_kv)

    grad_keys, grad_values, whole = pl.pallas_call(
        key_grad_kernel,
        out_shape=(sds((TOK, 256), BF), sds((TOK, 256), BF), sds((2, 8, 256), F32)),
        in_specs=[SMEM] + [VMEM] * 4,
        out_specs=(VMEM,) * 3,
        compiler_params=PARAMS,
        cost_estimate=cost(10**6, 4 * 10**6),
        name="key_grad",
    )(idx, dk, dv, mate_kv, far_kv)

    return normed, grad_queries, grad_keys, grad_values, whole


def solution(mesh):
    spec = P("seq", "head")
    return jax.shard_map(
        local,
        mesh=mesh,
        in_specs=(spec,) * 4,
        out_specs=(spec,) * 4 + (P(None, "seq", "head"),),
        check_vma=False,
    )
```

```python
import jax
import jax.numpy as jnp
from jax import lax
from jax.experimental import pallas as pl
from jax.experimental.pallas import tpu as pltpu
from jax.sharding import PartitionSpec as P

H = 16
HD = 128
D = H * HD
TOK = 1024
SEG = 512
NEG = -1e30
EPS = 1e-05
SCALE = HD ** (-0.5)
BF = jnp.bfloat16
F32 = jnp.float32
VMEM = pl.BlockSpec(memory_space=pltpu.VMEM)
SMEM = pl.BlockSpec(memory_space=pltpu.SMEM)
PARAMS = pltpu.CompilerParams(vmem_limit_bytes=16 * 1024 * 1024)


def dot_nt(a, b):
    return lax.dot_general(a, b, (((1,), (1,)), ((), ())), preferred_element_type=F32)


def dot_nn(a, b):
    return lax.dot_general(a, b, (((1,), (0,)), ((), ())), preferred_element_type=F32)


def dot_tn(a, b):
    return lax.dot_general(a, b, (((0,), (0,)), ((), ())), preferred_element_type=F32)


def iota(shape, axis):
    return lax.broadcasted_iota(jnp.int32, shape, axis)


def cost(flops, bytes_accessed, transcendentals=0):
    return pl.CostEstimate(
        flops=flops, bytes_accessed=bytes_accessed, transcendentals=transcendentals
    )


def split3(x):
    hi = x.astype(BF)
    rest = x - hi.astype(F32)
    mid = rest.astype(BF)
    low = (rest - mid.astype(F32)).astype(BF)
    return hi.astype(F32), mid.astype(F32), low.astype(F32)


def select_kernel(idx, q_ref, k_ref, v_ref, mid_ref, far_ref, wide):
    far = []
    for j in range(2):
        head = idx[1] * 2 + j
        for a, ref in enumerate((k_ref, v_ref, q_ref)):
            slot = wide.at[j * 3 + a]
            slot[...] = ref[:, j * HD : (j + 1) * HD].astype(F32)
            mid = slot[pl.ds(lax.rem(head, 8), 128, stride=8), :]
            mid_ref[j * 128 : (j + 1) * 128, a * HD : (a + 1) * HD] = mid.astype(BF)
            far.append(slot[pl.ds(head, 8, stride=128), :])
    for a in range(3):
        both = jnp.concatenate([far[a], far[3 + a]], 0)
        far_ref[:, a * HD : (a + 1) * HD] = both.astype(BF)


def near_forward_kernel(q_ref, k_ref, v_ref, o_ref, lse_ref):
    for c in range(2):
        rows = slice(c * 256, (c + 1) * 256)
        n = (c + 1) * 256
        s = dot_nt(q_ref[rows, :], k_ref[:n, :]) * SCALE
        keep = iota((256, n), 1) <= iota((256, n), 0) + c * 256
        s = jnp.where(keep, s, NEG)
        top = jnp.max(s, axis=1, keepdims=True)
        p = jnp.exp(s - top)
        total = jnp.sum(p, axis=1, keepdims=True)
        o = dot_nn(p.astype(BF), v_ref[:n, :])
        o_ref[0, rows, :] = o / total
        lse_ref[0, rows, :] = jnp.broadcast_to(top + jnp.log(total), (256, HD))


def mid_slots(s, shape, axis):
    n = iota(shape, axis)
    pos = n // 128
    other = s ^ ((pos & 1) * 2 + (pos >> 1))
    return (other & 3) * 128 + (n & 127)


def mid_forward_kernel(idx, mid_ref, o_ref, lse_ref):
    s_idx = idx[0]
    key_slot = mid_slots(s_idx, (128, SEG), 1)
    query_slot = (s_idx & 3) * 128 + iota((128, SEG), 0)
    keep = key_slot <= query_slot
    for j in range(2):
        q = mid_ref[j * 128 : (j + 1) * 128, 2 * HD :]
        k = jnp.concatenate(
            [mid_ref[p * 256 + j * 128 : p * 256 + (j + 1) * 128, :HD] for p in range(4)], 0
        )
        v = jnp.concatenate(
            [mid_ref[p * 256 + j * 128 : p * 256 + (j + 1) * 128, HD : 2 * HD] for p in range(4)], 0
        )
        s = jnp.where(keep, dot_nt(q, k) * SCALE, NEG)
        top = jnp.max(s, axis=1, keepdims=True)
        p = jnp.exp(s - top)
        total = jnp.sum(p, axis=1, keepdims=True)
        o = dot_nn(p.astype(BF), v)
        o_ref[j * 128 : (j + 1) * 128, :] = o / total
        lse_ref[j * 128 : (j + 1) * 128, :] = jnp.broadcast_to(top + jnp.log(total), (128, HD))


def far_places(s):
    n, row = iota((32, 1024), 1), iota((32, 1024), 0)
    pos = n // 32
    flips = (pos & 1) * 32 + (pos & 2) * 8 + (pos & 4) * 2 + ((pos & 8) >> 1) + ((pos & 16) >> 3)
    place = (((s | 1) ^ flips) - ((n >> 4) & 1)) * 8 + (n & 7)
    mine = ((s | 1) - (row >> 4)) * 8 + (row & 7)
    return ((n >> 3) & 1) == ((row >> 3) & 1), place, mine


def by_parity(idx, if_odd, if_even):
    odd = (iota(if_odd.shape, 0) * 0 + (idx[0] & 1)) == 1
    return jnp.where(odd, if_odd, if_even)


def far_keep_forward(s):
    same_head, place, mine = far_places(s)
    return same_head & (place <= mine)


def far_keep_backward(s):
    same_head, place, mine = far_places(s)
    return same_head & (place >= mine)


def pre_kernel(
    idx, o0, lse0, o1, lse1, mid_o, mid_lse, g_ref, att_ref, lse_ref, far_ref, out_scr
):
    for j in range(2):
        head = idx[1] * 2 + j
        picked = pl.ds(lax.rem(head, 8), 128, stride=8)
        distant = pl.ds(head, 8, stride=128)
        own = slice(j * 128, (j + 1) * 128)
        so, sl = out_scr.at[j], lse_ref.at[j]
        so[:SEG, :], so[SEG:, :] = o0[j], o1[j]
        sl[:SEG, :], sl[SEG:, :] = lse0[j], lse1[j]
        l1, l2 = sl[picked, :], mid_lse[own, :]
        peak = jnp.maximum(l1, l2)
        e1, e2 = jnp.exp(l1 - peak), jnp.exp(l2 - peak)
        den = e1 + e2
        so[picked, :] = (e1 * so[picked, :] + e2 * mid_o[own, :]) / den
        sl[picked, :] = peak + jnp.log(den)
        far_ref[j * 8 : (j + 1) * 8, :] = so[distant, :]
        far_ref[16 + j * 8 : 24 + j * 8, :] = sl[distant, :]
    lane = iota((128, HD), 1)
    row = iota((128, HD), 0)
    table = jnp.zeros((128, HD), F32)
    for b in range(8):
        rows = slice(b * 128, (b + 1) * 128)
        at, g = [], []
        for j in range(2):
            a16 = out_scr[j, rows, :].astype(BF)
            att_ref[rows, j * HD : (j + 1) * HD] = a16
            at.append(jnp.where(row == idx[1] * 2 + j, 0.0, a16.astype(F32)))
            g.append(g_ref[rows, j * HD : (j + 1) * HD].astype(F32))
            out_scr[j, rows, :] = g[j]
        sums = (
            at[0] + at[1],
            at[0] * at[0] + at[1] * at[1],
            g[0] * at[0] + g[1] * at[1],
            g[0] + g[1],
        )
        for i, term in enumerate(sums):
            table = jnp.where(lane == b * 4 + i, jnp.sum(term, axis=1, keepdims=True), table)
    far_ref[48:, :] = table.T[:32, :]
    for j in range(2):
        distant = pl.ds(idx[1] * 2 + j, 8, stride=128)
        far_ref[32 + j * 8 : 40 + j * 8, :] = out_scr.at[j][distant, :]


def norm_terms(total, squares, cross, g_total):
    mean = total / D
    rstd = lax.rsqrt(squares / D - mean * mean + EPS)
    return mean, rstd, g_total / D, rstd * (cross - mean * g_total) / D


def stat_pack(lse, delta, lane):
    pack = jnp.zeros(lane.shape, F32)
    for i, term in enumerate(split3(lse) + split3(delta)):
        pack = jnp.where(lane == i, term, pack)
    return pack


def far_kernel(idx, far_all, rows_ref, own_ref, mate_ref, packs_ref, fix_ref, col_scr):
    q = rows_ref[:, 2 * HD :]
    s = jnp.where(far_keep_forward(idx[0]), dot_nt(q, far_all[:, :HD]) * SCALE, NEG)
    top = jnp.max(s, axis=1, keepdims=True)
    p = jnp.exp(s - top)
    total = jnp.sum(p, axis=1, keepdims=True)
    o3 = dot_nn(p.astype(BF), far_all[:, HD : 2 * HD]) / total
    l3 = top + jnp.log(total)
    o12 = jnp.concatenate([own_ref[:16], mate_ref[:16]], 0)
    l12 = jnp.concatenate([own_ref[16:32], mate_ref[16:32]], 0)
    g = jnp.concatenate([own_ref[32:48], mate_ref[32:48]], 0)
    peak = jnp.maximum(l12, l3)
    e12, e3 = jnp.exp(l12 - peak), jnp.exp(l3 - peak)
    den = e12 + e3
    at16 = ((e12 * o12 + e3 * o3) / den).astype(BF)
    at = at16.astype(F32)
    lse = peak + jnp.log(den)

    others = [[], [], [], []]
    lane64 = iota((64, HD), 1)
    for half in range(2):
        for j in range(2):
            cs = col_scr.at[half * 2 + j]
            chosen = jnp.where(lane64 == idx[1] * 2 + j, mate_ref[48:], 0.0)
            cs[...] = jnp.broadcast_to(jnp.sum(chosen, axis=1, keepdims=True), (64, HD))
            for k in range(4):
                others[k].append(cs[pl.ds(half * 32 + k, 8, stride=4), :])
    others = [jnp.concatenate(part, 0) for part in others]
    lane, row = iota((32, HD), 1), iota((32, HD), 0)
    here = lane == (row & 7) * 16 + idx[1] * 2 + ((row >> 3) & 1)
    sums = []
    fix_ref[...] = jnp.zeros((8, HD), F32)
    for k, term in enumerate((at, at * at, g * at)):
        mine = jnp.sum(term, axis=1, keepdims=True)
        sums.append(others[k] + mine)
        placed = jnp.where(here, mine, 0.0)
        for half in range(2):
            own = placed[half * 16 : half * 16 + 16]
            fix_ref[half * 4 + k : half * 4 + k + 1, :] = jnp.sum(own, axis=0, keepdims=True)
    mean, rstd, sg, sgx = norm_terms(sums[0], sums[1], sums[2], others[3])
    x = (at - mean) * rstd
    grad = (rstd * (g - sg - x * sgx)).astype(BF)
    delta = jnp.sum(grad.astype(F32) * at, axis=1, keepdims=True)
    packs_ref[:32, :HD] = grad
    delta = jnp.broadcast_to(delta, (32, HD))
    packs_ref[:32, HD : 2 * HD] = stat_pack(lse, delta, lane).astype(BF)
    packs_ref[:32, 2 * HD :] = q
    packs_ref[32:, :HD] = at16
    packs_ref[32:, HD : 2 * HD] = at16
    packs_ref[32:, 2 * HD :] = at16


def stat_cols(pack):
    pack = pack.astype(F32)
    lse = pack[:, 0:1] + pack[:, 1:2] + pack[:, 2:3]
    delta = pack[:, 3:4] + pack[:, 4:5] + pack[:, 5:6]
    return lse, delta


def far_query_kernel(idx, far_all, packs, dq_ref):
    @pl.when((idx[0] & 1) == 0)
    def _():
        k_all, v_all = far_all[:, :HD], far_all[:, HD : 2 * HD]
        lse, delta = stat_cols(packs[:32, HD : 2 * HD])
        keep = far_keep_forward(idx[0])
        s = jnp.where(keep, dot_nt(packs[:32, 2 * HD :], k_all) * SCALE, NEG)
        p = jnp.exp(s - lse)
        ds = (p * (dot_nt(packs[:32, :HD], v_all) - delta)).astype(BF)
        dq_ref[...] = dot_nn(ds, k_all) * SCALE


def norm_kernel(
    idx,
    mate_ref,
    stat_ref,
    fix_own,
    fix_got,
    packs_own,
    packs_got,
    att_ref,
    g_ref,
    lse_in,
    normed_ref,
    grad_ref,
    delta_ref,
    lse_ref,
    mid_ref,
    att_scr,
    sum_scr,
):
    sums = by_parity(idx, mate_ref[48:80], stat_ref[32:])
    fixes = by_parity(idx, fix_own[:4], fix_got[4:])
    far_at = by_parity(
        idx, packs_own[32:48, :HD].astype(F32), packs_got[48:, :HD].astype(F32)
    )
    far_stat = by_parity(
        idx,
        packs_own[:16, HD : 2 * HD].astype(F32),
        packs_got[16:32, HD : 2 * HD].astype(F32),
    )
    far_lse = jnp.broadcast_to(stat_cols(far_stat)[0], (16, HD))
    for j in range(2):
        distant = pl.ds(idx[1] * 2 + j, 8, stride=128)
        at, lse = att_scr.at[j], lse_ref.at[j]
        at[...] = att_ref[:, j * HD : (j + 1) * HD].astype(F32)
        at[distant, :] = far_at[j * 8 : j * 8 + 8]
        lse[...] = lse_in[j]
        lse[distant, :] = far_lse[j * 8 : j * 8 + 8]
    for b in range(8):
        fix = jnp.concatenate(
            [fixes[:, b * 16 : (b + 1) * 16], jnp.zeros((4, HD - 16), F32)], 1
        )
        sum_scr[b * 4 : b * 4 + 4, :] = sums[b * 4 : b * 4 + 4] + fix
    terms = norm_terms(*(sum_scr[pl.ds(k, 8, stride=4), :] for k in range(4)))
    cols = jnp.concatenate(list(terms) + [jnp.zeros((96, HD), F32)], 0).T
    for b in range(8):
        rows = slice(b * 128, (b + 1) * 128)
        mean, rstd, sg, sgx = (cols[:, i * 8 + b : i * 8 + b + 1] for i in range(4))
        for j in range(2):
            at = att_scr[j, rows, :]
            x = (at - mean) * rstd
            normed_ref[rows, j * HD : (j + 1) * HD] = x.astype(BF)
            g = g_ref[rows, j * HD : (j + 1) * HD].astype(F32)
            grad = (rstd * (g - sg - x * sgx)).astype(BF)
            grad_ref[rows, j * HD : (j + 1) * HD] = grad
            grad = grad.astype(F32)
            delta = jnp.sum(grad * at, axis=1, keepdims=True)
            delta_ref[j, rows, :] = jnp.broadcast_to(delta, (128, HD))
            att_scr[j, rows, :] = grad
    lane = iota((128, HD), 1)
    for j in range(2):
        picked = pl.ds(lax.rem(idx[1] * 2 + j, 8), 128, stride=8)
        own = slice(j * 128, (j + 1) * 128)
        mid_ref[own, :HD] = att_scr.at[j][picked, :].astype(BF)
        pack = stat_pack(lse_ref.at[j][picked, :], delta_ref.at[j][picked, :], lane)
        mid_ref[own, HD:] = pack.astype(BF)


def near_backward_kernel(
    q_ref, k_ref, v_ref, g_ref, lse_ref, delta_ref, dq_ref, dk_ref, dv_ref
):
    for c in range(2):
        keys = slice(c * 256, (c + 1) * 256)
        rows = slice(c * 256, 512)
        n = 512 - c * 256
        q, g = q_ref[rows, :], g_ref[rows, :]
        k, v = k_ref[keys, :], v_ref[keys, :]
        lse = jnp.concatenate([lse_ref[0, rows, :]] * 2, 1)
        delta = jnp.concatenate([delta_ref[0, rows, :]] * 2, 1)
        s = dot_nt(q, k) * SCALE
        keep = iota((n, 256), 1) <= iota((n, 256), 0)
        p = jnp.exp(jnp.where(keep, s, NEG) - lse)
        ds = (p * (dot_nt(g, v) - delta)).astype(BF)
        p = p.astype(BF)
        dv_ref[0, keys, :] = dot_tn(p, g)
        dk_ref[0, keys, :] = dot_tn(ds, q) * SCALE
        dq = dot_nn(ds, k) * SCALE
        if c == 0:
            dq_ref[0, :, :] = dq
        else:
            dq_ref[0, rows, :] += dq


def query_grad_kernel(idx, dq0, dq1, mid_ref, mid_g, far_got, far_own, out_ref, scr, far_scr):
    s_idx = idx[0]
    far_dq = by_parity(idx, far_got[64:80], far_own[80:])
    key_slot = mid_slots(s_idx, (128, SEG), 1)
    query_slot = (s_idx & 3) * 128 + iota((128, SEG), 0)
    keep = key_slot <= query_slot
    for j in range(2):
        head = idx[1] * 2 + j
        own = slice(j * 128, (j + 1) * 128)
        q = mid_ref[own, 2 * HD :]
        g = mid_g[own, :HD]
        lse, delta = stat_cols(mid_g[own, HD:])
        k = jnp.concatenate(
            [mid_ref[p * 256 + j * 128 : p * 256 + (j + 1) * 128, :HD] for p in range(4)], 0
        )
        v = jnp.concatenate(
            [mid_ref[p * 256 + j * 128 : p * 256 + (j + 1) * 128, HD : 2 * HD] for p in range(4)], 0
        )
        s = jnp.where(keep, dot_nt(q, k) * SCALE, NEG)
        p = jnp.exp(s - lse)
        ds = (p * (dot_nt(g, v) - delta)).astype(BF)
        fs = far_scr.at[j]
        fs[...] = dot_nn(ds, k) * SCALE
        spread = pl.ds(head // 8, 8, stride=16)
        fs[spread, :] = fs[spread, :] + far_dq[j * 8 : (j + 1) * 8]
        picked = pl.ds(lax.rem(head, 8), 128, stride=8)
        sc = scr.at[j]
        sc[:SEG, :], sc[SEG:, :] = dq0[j], dq1[j]
        sc[picked, :] = sc[picked, :] + fs[...]
        out_ref[:, j * HD : (j + 1) * HD] = sc[...].astype(BF)


def stat_rows(packs):
    lane, row = iota((8, HD), 1), iota((8, HD), 0)
    pick = ((row == lane // 3) & (lane < 6)).astype(F32).astype(BF)
    stats = dot_nt(pick, packs)
    return stats[0:1], stats[1:2]


def far_key_kernel(idx, far_all, grads, dq_ref, out_ref):
    @pl.when((idx[0] & 1) == 0)
    def _():
        lse, delta = stat_rows(grads[:, HD : 2 * HD])
        k, v = far_all[:32, :HD], far_all[:32, HD : 2 * HD]
        q_all, g_all = grads[:, 2 * HD :], grads[:, :HD]
        s = jnp.where(far_keep_backward(idx[0]), dot_nt(k, q_all) * SCALE, NEG)
        p = jnp.exp(s - lse)
        ds = (p * (dot_nt(v, g_all) - delta)).astype(BF)
        out_ref[:32, :] = dot_nn(ds, q_all) * SCALE
        out_ref[32:64, :] = dot_nn(p.astype(BF), g_all)
        out_ref[64:, :] = dq_ref[...]


def mid_key_kernel(idx, dk0, dk1, dv0, dv1, mid_ref, grads, dk_ref, dv_ref):
    s_idx = idx[0]
    all_lse, all_delta = stat_rows(grads[:, HD:])
    query_slot = mid_slots(s_idx, (128, SEG), 1)
    key_slot = (s_idx & 3) * 128 + iota((128, SEG), 0)
    keep = key_slot <= query_slot
    for j in range(2):
        own = slice(j * 128, (j + 1) * 128)
        places = [slice(p * 256 + j * 128, p * 256 + (j + 1) * 128) for p in range(4)]
        k, v = mid_ref[own, :HD], mid_ref[own, HD : 2 * HD]
        q = jnp.concatenate([mid_ref[r, 2 * HD :] for r in places], 0)
        g = jnp.concatenate([grads[r, :HD] for r in places], 0)
        lse = jnp.concatenate([all_lse[:, r] for r in places], 1)
        delta = jnp.concatenate([all_delta[:, r] for r in places], 1)
        s = jnp.where(keep, dot_nt(k, q) * SCALE, NEG)
        p = jnp.exp(s - lse)
        ds = (p * (dot_nt(v, g) - delta)).astype(BF)
        picked = pl.ds(lax.rem(idx[1] * 2 + j, 8), 128, stride=8)
        for near0, near1, mid, out_ref in (
            (dk0, dk1, dot_nn(ds, q) * SCALE, dk_ref),
            (dv0, dv1, dot_nn(p.astype(BF), g), dv_ref),
        ):
            out = out_ref.at[j]
            out[:SEG, :], out[SEG:, :] = near0[j], near1[j]
            out[picked, :] = out[picked, :] + mid


def key_grad_kernel(idx, dk_in, dv_in, far_got, far_own, dk_out, dv_out, whole_ref):
    row = iota((128, HD), 0)
    for j in range(2):
        here = row == idx[1] * 2 + j
        cols = slice(j * HD, (j + 1) * HD)
        for a, (near, out) in enumerate(((dk_in, dk_out), (dv_in, dv_out))):
            first = a * 32 + j * 8
            far = by_parity(idx, far_got[first : first + 8], far_own[first + 16 : first + 24])
            whole_ref[a, :, cols] = far
            for b in range(8):
                rows = slice(b * 128, (b + 1) * 128)
                total = near[j, rows, :] + jnp.where(here, far[b : b + 1], 0.0)
                out[rows, cols] = total.astype(BF)


def exchange(x, bit):
    return lax.ppermute(x, "seq", [(i, i ^ bit) for i in range(64)])


def chip_exchange(x, bit, parity):
    return lax.ppermute(x, "seq", [(i, i ^ bit) for i in range(parity, 64, 2)])


def head_exchange(x, bit, parity):
    pairs = [(s * 8 + h, s * 8 + (h ^ bit)) for s in range(parity, 64, 2) for h in range(8)]
    return lax.ppermute(x, ("seq", "head"), pairs)


def to_odd(x):
    return lax.ppermute(x, "seq", [(i, i + 1) for i in range(0, 64, 2)])


def to_even(x):
    return lax.ppermute(x, "seq", [(i + 1, i) for i in range(0, 64, 2)])


def joined(a, b):
    return jnp.concatenate([a, b], 0)


def after(arrays):
    return lax.optimization_barrier(arrays)


def sds(shape, dtype):
    return jax.ShapeDtypeStruct(shape, dtype)


def local(queries, keys, values, out_grad):
    seq_index = lax.axis_index("seq")
    head_index = lax.axis_index("head")
    idx = jnp.stack([seq_index, head_index]).astype(jnp.int32)

    mid0, far0 = pl.pallas_call(
        select_kernel,
        out_shape=(sds((256, 384), BF), sds((16, 384), BF)),
        in_specs=[SMEM, VMEM, VMEM, VMEM],
        out_specs=(VMEM, VMEM),
        scratch_shapes=[pltpu.VMEM((6, TOK, HD), F32)],
        compiler_params=PARAMS,
        cost_estimate=cost(10**6, 2 * 10**6),
        name="select",
    )(idx, queries, keys, values)

    unit = pl.BlockSpec((SEG, HD), lambda b, j: (b, j))
    by_head = pl.BlockSpec((1, SEG, HD), lambda b, j: (j, b, 0))
    by_head_shape = sds((2, TOK, HD), F32)
    half = pl.BlockSpec((1, SEG, HD), lambda j: (j, 0, 0))
    half_shape = sds((2, SEG, HD), F32)

    def near_forward(block):
        part = pl.BlockSpec((SEG, HD), lambda j: (block, j))
        return pl.pallas_call(
            near_forward_kernel,
            grid=(2,),
            out_shape=(half_shape, half_shape),
            in_specs=[part, part, part],
            out_specs=(half, half),
            compiler_params=PARAMS,
            cost_estimate=cost(4 * 10**8, 2 * 10**6, 10**6),
            name=f"near_forward_{block}",
        )(queries, keys, values)

    mid1 = exchange(mid0, 2)
    mate_far = to_odd(far0)
    near0, near1 = near_forward(0), near_forward(1)
    mid_two, far1, near0, near1 = after(
        (joined(mid0, mid1), joined(far0, mate_far), near0, near1)
    )
    mid2 = exchange(mid_two, 1)
    mid_all = joined(mid_two, mid2)
    mid_o, mid_lse = pl.pallas_call(
        mid_forward_kernel,
        out_shape=(sds((256, HD), F32), sds((256, HD), F32)),
        in_specs=[SMEM, VMEM],
        out_specs=(VMEM, VMEM),
        compiler_params=PARAMS,
        cost_estimate=cost(2 * 10**8, 10**6, 10**5),
        name="mid_forward",
    )(idx, mid_all)

    att, lse12, bundle = pl.pallas_call(
        pre_kernel,
        out_shape=(sds((TOK, 256), BF), by_head_shape, sds((80, HD), F32)),
        in_specs=[SMEM] + [VMEM] * 7,
        out_specs=(VMEM,) * 3,
        scratch_shapes=[pltpu.VMEM((2, TOK, HD), F32)],
        compiler_params=PARAMS,
        cost_estimate=cost(10**7, 4 * 10**6, 10**5),
        name="pre",
    )(idx, *near0, *near1, mid_o, mid_lse, out_grad)
    rows, bundle = after((far1, bundle))
    far1 = rows[:, : 2 * HD]
    mate_stats = to_even(bundle[48:])
    from1 = chip_exchange(far1, 32, 1)
    stats = joined(mate_stats, bundle[48:])
    sums1 = head_exchange(stats, 2, 0)
    far2, stats = after((joined(far1, from1), stats + sums1))
    from2 = chip_exchange(far2, 16, 1)
    sums2 = head_exchange(stats, 1, 0)
    far4, stats = after((joined(far2, from2), stats + sums2))
    from4 = chip_exchange(far4, 8, 1)
    sums3 = head_exchange(stats, 4, 0)
    far8 = joined(far4, from4)
    from8 = chip_exchange(far8, 4, 1)
    far16 = joined(far8, from8)
    from16 = chip_exchange(far16, 2, 1)
    stats = stats + sums3
    mate = to_odd(joined(bundle[:48], stats))
    far_all = joined(far16, from16)
    far_all, mate = after((far_all, mate))
    far_even = to_even(far_all)

    packs, fix = pl.pallas_call(
        far_kernel,
        out_shape=(sds((64, 384), BF), sds((8, HD), F32)),
        in_specs=[SMEM] + [VMEM] * 4,
        out_specs=(VMEM,) * 2,
        scratch_shapes=[pltpu.VMEM((4, 64, HD), F32)],
        compiler_params=PARAMS,
        cost_estimate=cost(10**7, 10**6, 10**5),
        name="far",
    )(idx, far_all, rows, bundle, mate)

    packs_even = to_even(packs)
    fix1 = head_exchange(fix, 2, 1)
    part0, fix = after((packs_even[:32], fix + fix1))
    part1 = chip_exchange(part0, 32, 0)
    fix2 = head_exchange(fix, 1, 1)
    part_a, fix = after((joined(part0, part1), fix + fix2))
    part2 = chip_exchange(part_a, 16, 0)
    fix3 = head_exchange(fix, 4, 1)
    far_dq = pl.pallas_call(
        far_query_kernel,
        out_shape=sds((32, HD), F32),
        in_specs=[SMEM] + [VMEM] * 2,
        out_specs=VMEM,
        compiler_params=PARAMS,
        cost_estimate=cost(10**7, 10**6, 10**5),
        name="far_query",
    )(idx, far_even, packs_even)
    part_b, fix = after((joined(part_a, part2), fix + fix3))
    part3 = chip_exchange(part_b, 8, 0)
    part_c, far_dq = after((joined(part_b, part3), far_dq))
    part4 = chip_exchange(part_c, 4, 0)
    part_c, fix_sent = after((part_c, fix))
    fix_even = to_even(fix_sent)
    normed, grad, delta, lse, mid_g = pl.pallas_call(
        norm_kernel,
        out_shape=(
            sds((TOK, 256), BF),
            sds((TOK, 256), BF),
            by_head_shape,
            by_head_shape,
            sds((256, 256), BF),
        ),
        in_specs=[SMEM] + [VMEM] * 9,
        out_specs=(VMEM,) * 5,
        scratch_shapes=[pltpu.VMEM((2, TOK, HD), F32), pltpu.VMEM((32, HD), F32)],
        compiler_params=PARAMS,
        cost_estimate=cost(10**7, 4 * 10**6),
        name="norm",
    )(idx, mate, stats, fix, fix_even, packs, packs_even, att, out_grad, lse12)

    def near_backward(block):
        part = pl.BlockSpec((SEG, HD), lambda j: (block, j))
        stat = pl.BlockSpec((1, SEG, HD), lambda j: (j, block, 0))
        return pl.pallas_call(
            near_backward_kernel,
            grid=(2,),
            out_shape=(half_shape,) * 3,
            in_specs=[part] * 4 + [stat] * 2,
            out_specs=(half,) * 3,
            compiler_params=PARAMS,
            cost_estimate=cost(10**9, 4 * 10**6, 10**6),
            name=f"near_backward_{block}",
        )(queries, keys, values, grad, lse, delta)

    mid_g1 = exchange(mid_g, 2)
    part_d, grad = after((joined(part_c, part4), grad))
    part5 = chip_exchange(part_d, 2, 0)
    dq0, dk0, dv0 = near_backward(0)
    dq1, dk1, dv1 = near_backward(1)
    mid_gs, far_gs, dq0, dq1 = after(
        (joined(mid_g, mid_g1), joined(part_d, part5), dq0, dq1)
    )
    mid_g2 = exchange(mid_gs, 1)

    far_kv = pl.pallas_call(
        far_key_kernel,
        out_shape=sds((96, HD), F32),
        in_specs=[SMEM] + [VMEM] * 3,
        out_specs=VMEM,
        compiler_params=PARAMS,
        cost_estimate=cost(10**7, 10**6, 10**5),
        name="far_key",
    )(idx, far_even, far_gs, far_dq)
    mate_kv = to_odd(far_kv)

    mid_gall = joined(mid_gs, mid_g2)
    dk, dv = pl.pallas_call(
        mid_key_kernel,
        out_shape=(by_head_shape, by_head_shape),
        in_specs=[SMEM] + [VMEM] * 6,
        out_specs=(VMEM,) * 2,
        compiler_params=PARAMS,
        cost_estimate=cost(2 * 10**8, 4 * 10**6, 10**5),
        name="mid_key",
    )(idx, dk0, dk1, dv0, dv1, mid_all, mid_gall)
    mate_kv, dk = after((mate_kv, dk))

    grad_queries = pl.pallas_call(
        query_grad_kernel,
        out_shape=sds((TOK, 256), BF),
        in_specs=[SMEM] + [VMEM] * 6,
        out_specs=VMEM,
        scratch_shapes=[pltpu.VMEM((2, TOK, HD), F32), pltpu.VMEM((2, 128, HD), F32)],
        compiler_params=PARAMS,
        cost_estimate=cost(2 * 10**8, 3 * 10**6, 10**5),
        name="query_grad",
    )(idx, dq0, dq1, mid_all, mid_g, mate_kv, far_kv)

    grad_keys, grad_values, whole = pl.pallas_call(
        key_grad_kernel,
        out_shape=(sds((TOK, 256), BF), sds((TOK, 256), BF), sds((2, 8, 256), F32)),
        in_specs=[SMEM] + [VMEM] * 4,
        out_specs=(VMEM,) * 3,
        compiler_params=PARAMS,
        cost_estimate=cost(10**6, 4 * 10**6),
        name="key_grad",
    )(idx, dk, dv, mate_kv, far_kv)

    return normed, grad_queries, grad_keys, grad_values, whole


def solution(mesh):
    spec = P("seq", "head")
    return jax.shard_map(
        local,
        mesh=mesh,
        in_specs=(spec,) * 4,
        out_specs=(spec,) * 4 + (P(None, "seq", "head"),),
        check_vma=False,
    )
```

```python
import jax
import jax.numpy as jnp
from jax import lax
from jax.experimental import pallas as pl
from jax.experimental.pallas import tpu as pltpu
from jax.sharding import PartitionSpec as P

H = 16
HD = 128
D = H * HD
TOK = 1024
SEG = 512
NEG = -1e30
EPS = 1e-05
SCALE = HD ** (-0.5)
BF = jnp.bfloat16
F32 = jnp.float32
VMEM = pl.BlockSpec(memory_space=pltpu.VMEM)
SMEM = pl.BlockSpec(memory_space=pltpu.SMEM)
PARAMS = pltpu.CompilerParams(vmem_limit_bytes=16 * 1024 * 1024)


def dot_nt(a, b):
    return lax.dot_general(a, b, (((1,), (1,)), ((), ())), preferred_element_type=F32)


def dot_nn(a, b):
    return lax.dot_general(a, b, (((1,), (0,)), ((), ())), preferred_element_type=F32)


def dot_tn(a, b):
    return lax.dot_general(a, b, (((0,), (0,)), ((), ())), preferred_element_type=F32)


def iota(shape, axis):
    return lax.broadcasted_iota(jnp.int32, shape, axis)


def cost(flops, bytes_accessed, transcendentals=0):
    return pl.CostEstimate(
        flops=flops, bytes_accessed=bytes_accessed, transcendentals=transcendentals
    )


def split3(x):
    hi = x.astype(BF)
    rest = x - hi.astype(F32)
    mid = rest.astype(BF)
    low = (rest - mid.astype(F32)).astype(BF)
    return hi.astype(F32), mid.astype(F32), low.astype(F32)


def select_kernel(idx, q_ref, k_ref, v_ref, mid_ref, far_ref, wide):
    far = []
    for j in range(2):
        head = idx[1] * 2 + j
        for a, ref in enumerate((k_ref, v_ref, q_ref)):
            slot = wide.at[j * 3 + a]
            slot[...] = ref[:, j * HD : (j + 1) * HD].astype(F32)
            mid = slot[pl.ds(lax.rem(head, 8), 128, stride=8), :]
            mid_ref[j * 128 : (j + 1) * 128, a * HD : (a + 1) * HD] = mid.astype(BF)
            far.append(slot[pl.ds(head, 8, stride=128), :])
    for a in range(3):
        both = jnp.concatenate([far[a], far[3 + a]], 0)
        far_ref[:, a * HD : (a + 1) * HD] = both.astype(BF)


def near_forward_kernel(q_ref, k_ref, v_ref, o_ref, lse_ref):
    for c in range(2):
        rows = slice(c * 256, (c + 1) * 256)
        n = (c + 1) * 256
        s = dot_nt(q_ref[rows, :], k_ref[:n, :]) * SCALE
        keep = iota((256, n), 1) <= iota((256, n), 0) + c * 256
        s = jnp.where(keep, s, NEG)
        top = jnp.max(s, axis=1, keepdims=True)
        p = jnp.exp(s - top)
        total = jnp.sum(p, axis=1, keepdims=True)
        o = dot_nn(p.astype(BF), v_ref[:n, :])
        o_ref[0, rows, :] = o / total
        lse_ref[0, rows, :] = jnp.broadcast_to(top + jnp.log(total), (256, HD))


def mid_slots(s, shape, axis):
    n = iota(shape, axis)
    pos = n // 128
    other = s ^ ((pos & 1) * 2 + (pos >> 1))
    return (other & 3) * 128 + (n & 127)


def mid_forward_kernel(idx, mid_ref, o_ref, lse_ref):
    s_idx = idx[0]
    key_slot = mid_slots(s_idx, (128, SEG), 1)
    query_slot = (s_idx & 3) * 128 + iota((128, SEG), 0)
    keep = key_slot <= query_slot
    for j in range(2):
        q = mid_ref[j * 128 : (j + 1) * 128, 2 * HD :]
        k = jnp.concatenate(
            [mid_ref[p * 256 + j * 128 : p * 256 + (j + 1) * 128, :HD] for p in range(4)], 0
        )
        v = jnp.concatenate(
            [mid_ref[p * 256 + j * 128 : p * 256 + (j + 1) * 128, HD : 2 * HD] for p in range(4)], 0
        )
        s = jnp.where(keep, dot_nt(q, k) * SCALE, NEG)
        top = jnp.max(s, axis=1, keepdims=True)
        p = jnp.exp(s - top)
        total = jnp.sum(p, axis=1, keepdims=True)
        o = dot_nn(p.astype(BF), v)
        o_ref[j * 128 : (j + 1) * 128, :] = o / total
        lse_ref[j * 128 : (j + 1) * 128, :] = jnp.broadcast_to(top + jnp.log(total), (128, HD))


def far_places(s):
    n, row = iota((32, 1024), 1), iota((32, 1024), 0)
    pos = n // 32
    flips = (pos & 1) * 32 + (pos & 2) * 8 + (pos & 4) * 2 + ((pos & 8) >> 1) + ((pos & 16) >> 3)
    place = (((s | 1) ^ flips) - ((n >> 4) & 1)) * 8 + (n & 7)
    mine = ((s | 1) - (row >> 4)) * 8 + (row & 7)
    return ((n >> 3) & 1) == ((row >> 3) & 1), place, mine


def by_parity(idx, if_odd, if_even):
    odd = (iota(if_odd.shape, 0) * 0 + (idx[0] & 1)) == 1
    return jnp.where(odd, if_odd, if_even)


def far_keep_forward(s):
    same_head, place, mine = far_places(s)
    return same_head & (place <= mine)


def far_keep_backward(s):
    same_head, place, mine = far_places(s)
    return same_head & (place >= mine)


def pre_kernel(
    idx, o0, lse0, o1, lse1, mid_o, mid_lse, g_ref, att_ref, lse_ref, far_ref, out_scr
):
    for j in range(2):
        head = idx[1] * 2 + j
        picked = pl.ds(lax.rem(head, 8), 128, stride=8)
        distant = pl.ds(head, 8, stride=128)
        own = slice(j * 128, (j + 1) * 128)
        so, sl = out_scr.at[j], lse_ref.at[j]
        so[:SEG, :], so[SEG:, :] = o0[j], o1[j]
        sl[:SEG, :], sl[SEG:, :] = lse0[j], lse1[j]
        l1, l2 = sl[picked, :], mid_lse[own, :]
        peak = jnp.maximum(l1, l2)
        e1, e2 = jnp.exp(l1 - peak), jnp.exp(l2 - peak)
        den = e1 + e2
        so[picked, :] = (e1 * so[picked, :] + e2 * mid_o[own, :]) / den
        sl[picked, :] = peak + jnp.log(den)
        far_ref[j * 8 : (j + 1) * 8, :] = so[distant, :]
        far_ref[16 + j * 8 : 24 + j * 8, :] = sl[distant, :]
    lane = iota((128, HD), 1)
    row = iota((128, HD), 0)
    table = jnp.zeros((128, HD), F32)
    for b in range(8):
        rows = slice(b * 128, (b + 1) * 128)
        at, g = [], []
        for j in range(2):
            a16 = out_scr[j, rows, :].astype(BF)
            att_ref[rows, j * HD : (j + 1) * HD] = a16
            at.append(jnp.where(row == idx[1] * 2 + j, 0.0, a16.astype(F32)))
            g.append(g_ref[rows, j * HD : (j + 1) * HD].astype(F32))
            out_scr[j, rows, :] = g[j]
        sums = (
            at[0] + at[1],
            at[0] * at[0] + at[1] * at[1],
            g[0] * at[0] + g[1] * at[1],
            g[0] + g[1],
        )
        for i, term in enumerate(sums):
            table = jnp.where(lane == b * 4 + i, jnp.sum(term, axis=1, keepdims=True), table)
    far_ref[48:, :] = table.T[:32, :]
    for j in range(2):
        distant = pl.ds(idx[1] * 2 + j, 8, stride=128)
        far_ref[32 + j * 8 : 40 + j * 8, :] = out_scr.at[j][distant, :]


def norm_terms(total, squares, cross, g_total):
    mean = total / D
    rstd = lax.rsqrt(squares / D - mean * mean + EPS)
    return mean, rstd, g_total / D, rstd * (cross - mean * g_total) / D


def stat_pack(lse, delta, lane):
    pack = jnp.zeros(lane.shape, F32)
    for i, term in enumerate(split3(lse) + split3(delta)):
        pack = jnp.where(lane == i, term, pack)
    return pack


def far_kernel(idx, far_all, rows_ref, own_ref, mate_ref, packs_ref, fix_ref, col_scr):
    q = rows_ref[:, 2 * HD :]
    s = jnp.where(far_keep_forward(idx[0]), dot_nt(q, far_all[:, :HD]) * SCALE, NEG)
    top = jnp.max(s, axis=1, keepdims=True)
    p = jnp.exp(s - top)
    total = jnp.sum(p, axis=1, keepdims=True)
    o3 = dot_nn(p.astype(BF), far_all[:, HD : 2 * HD]) / total
    l3 = top + jnp.log(total)
    o12 = jnp.concatenate([own_ref[:16], mate_ref[:16]], 0)
    l12 = jnp.concatenate([own_ref[16:32], mate_ref[16:32]], 0)
    g = jnp.concatenate([own_ref[32:48], mate_ref[32:48]], 0)
    peak = jnp.maximum(l12, l3)
    e12, e3 = jnp.exp(l12 - peak), jnp.exp(l3 - peak)
    den = e12 + e3
    at16 = ((e12 * o12 + e3 * o3) / den).astype(BF)
    at = at16.astype(F32)
    lse = peak + jnp.log(den)

    others = [[], [], [], []]
    lane64 = iota((64, HD), 1)
    for half in range(2):
        for j in range(2):
            cs = col_scr.at[half * 2 + j]
            chosen = jnp.where(lane64 == idx[1] * 2 + j, mate_ref[48:], 0.0)
            cs[...] = jnp.broadcast_to(jnp.sum(chosen, axis=1, keepdims=True), (64, HD))
            for k in range(4):
                others[k].append(cs[pl.ds(half * 32 + k, 8, stride=4), :])
    others = [jnp.concatenate(part, 0) for part in others]
    lane, row = iota((32, HD), 1), iota((32, HD), 0)
    here = lane == (row & 7) * 16 + idx[1] * 2 + ((row >> 3) & 1)
    sums = []
    fix_ref[...] = jnp.zeros((8, HD), F32)
    for k, term in enumerate((at, at * at, g * at)):
        mine = jnp.sum(term, axis=1, keepdims=True)
        sums.append(others[k] + mine)
        placed = jnp.where(here, mine, 0.0)
        for half in range(2):
            own = placed[half * 16 : half * 16 + 16]
            fix_ref[half * 4 + k : half * 4 + k + 1, :] = jnp.sum(own, axis=0, keepdims=True)
    mean, rstd, sg, sgx = norm_terms(sums[0], sums[1], sums[2], others[3])
    x = (at - mean) * rstd
    grad = (rstd * (g - sg - x * sgx)).astype(BF)
    delta = jnp.sum(grad.astype(F32) * at, axis=1, keepdims=True)
    packs_ref[:32, :HD] = grad
    delta = jnp.broadcast_to(delta, (32, HD))
    packs_ref[:32, HD : 2 * HD] = stat_pack(lse, delta, lane).astype(BF)
    packs_ref[:32, 2 * HD :] = q
    packs_ref[32:, :HD] = at16
    packs_ref[32:, HD : 2 * HD] = at16
    packs_ref[32:, 2 * HD :] = at16


def stat_cols(pack):
    pack = pack.astype(F32)
    lse = pack[:, 0:1] + pack[:, 1:2] + pack[:, 2:3]
    delta = pack[:, 3:4] + pack[:, 4:5] + pack[:, 5:6]
    return lse, delta


def far_query_kernel(idx, far_all, packs, dq_ref):
    @pl.when((idx[0] & 1) == 0)
    def _():
        k_all, v_all = far_all[:, :HD], far_all[:, HD : 2 * HD]
        lse, delta = stat_cols(packs[:32, HD : 2 * HD])
        keep = far_keep_forward(idx[0])
        s = jnp.where(keep, dot_nt(packs[:32, 2 * HD :], k_all) * SCALE, NEG)
        p = jnp.exp(s - lse)
        ds = (p * (dot_nt(packs[:32, :HD], v_all) - delta)).astype(BF)
        dq_ref[...] = dot_nn(ds, k_all) * SCALE


def norm_kernel(
    idx,
    mate_ref,
    stat_ref,
    fix_own,
    fix_got,
    packs_own,
    packs_got,
    att_ref,
    g_ref,
    lse_in,
    normed_ref,
    grad_ref,
    delta_ref,
    lse_ref,
    mid_ref,
    att_scr,
    sum_scr,
):
    sums = by_parity(idx, mate_ref[48:80], stat_ref[32:])
    fixes = by_parity(idx, fix_own[:4], fix_got[4:])
    far_at = by_parity(
        idx, packs_own[32:48, :HD].astype(F32), packs_got[48:, :HD].astype(F32)
    )
    far_stat = by_parity(
        idx,
        packs_own[:16, HD : 2 * HD].astype(F32),
        packs_got[16:32, HD : 2 * HD].astype(F32),
    )
    far_lse = jnp.broadcast_to(stat_cols(far_stat)[0], (16, HD))
    for j in range(2):
        distant = pl.ds(idx[1] * 2 + j, 8, stride=128)
        at, lse = att_scr.at[j], lse_ref.at[j]
        at[...] = att_ref[:, j * HD : (j + 1) * HD].astype(F32)
        at[distant, :] = far_at[j * 8 : j * 8 + 8]
        lse[...] = lse_in[j]
        lse[distant, :] = far_lse[j * 8 : j * 8 + 8]
    for b in range(8):
        fix = jnp.concatenate(
            [fixes[:, b * 16 : (b + 1) * 16], jnp.zeros((4, HD - 16), F32)], 1
        )
        sum_scr[b * 4 : b * 4 + 4, :] = sums[b * 4 : b * 4 + 4] + fix
    terms = norm_terms(*(sum_scr[pl.ds(k, 8, stride=4), :] for k in range(4)))
    cols = jnp.concatenate(list(terms) + [jnp.zeros((96, HD), F32)], 0).T
    for b in range(8):
        rows = slice(b * 128, (b + 1) * 128)
        mean, rstd, sg, sgx = (cols[:, i * 8 + b : i * 8 + b + 1] for i in range(4))
        for j in range(2):
            at = att_scr[j, rows, :]
            x = (at - mean) * rstd
            normed_ref[rows, j * HD : (j + 1) * HD] = x.astype(BF)
            g = g_ref[rows, j * HD : (j + 1) * HD].astype(F32)
            grad = (rstd * (g - sg - x * sgx)).astype(BF)
            grad_ref[rows, j * HD : (j + 1) * HD] = grad
            grad = grad.astype(F32)
            delta = jnp.sum(grad * at, axis=1, keepdims=True)
            delta_ref[j, rows, :] = jnp.broadcast_to(delta, (128, HD))
            att_scr[j, rows, :] = grad
    lane = iota((128, HD), 1)
    for j in range(2):
        picked = pl.ds(lax.rem(idx[1] * 2 + j, 8), 128, stride=8)
        own = slice(j * 128, (j + 1) * 128)
        mid_ref[own, :HD] = att_scr.at[j][picked, :].astype(BF)
        pack = stat_pack(lse_ref.at[j][picked, :], delta_ref.at[j][picked, :], lane)
        mid_ref[own, HD:] = pack.astype(BF)


def near_backward_kernel(
    q_ref, k_ref, v_ref, g_ref, lse_ref, delta_ref, dq_ref, dk_ref, dv_ref
):
    for c in range(2):
        keys = slice(c * 256, (c + 1) * 256)
        rows = slice(c * 256, 512)
        n = 512 - c * 256
        q, g = q_ref[rows, :], g_ref[rows, :]
        k, v = k_ref[keys, :], v_ref[keys, :]
        lse = jnp.concatenate([lse_ref[0, rows, :]] * 2, 1)
        delta = jnp.concatenate([delta_ref[0, rows, :]] * 2, 1)
        s = dot_nt(q, k) * SCALE
        keep = iota((n, 256), 1) <= iota((n, 256), 0)
        p = jnp.exp(jnp.where(keep, s, NEG) - lse)
        ds = (p * (dot_nt(g, v) - delta)).astype(BF)
        p = p.astype(BF)
        dv_ref[0, keys, :] = dot_tn(p, g)
        dk_ref[0, keys, :] = dot_tn(ds, q) * SCALE
        dq = dot_nn(ds, k) * SCALE
        if c == 0:
            dq_ref[0, :, :] = dq
        else:
            dq_ref[0, rows, :] += dq


def query_grad_kernel(idx, dq0, dq1, mid_ref, mid_g, far_got, far_own, out_ref, scr, far_scr):
    s_idx = idx[0]
    far_dq = by_parity(idx, far_got[64:80], far_own[80:])
    key_slot = mid_slots(s_idx, (128, SEG), 1)
    query_slot = (s_idx & 3) * 128 + iota((128, SEG), 0)
    keep = key_slot <= query_slot
    for j in range(2):
        head = idx[1] * 2 + j
        own = slice(j * 128, (j + 1) * 128)
        q = mid_ref[own, 2 * HD :]
        g = mid_g[own, :HD]
        lse, delta = stat_cols(mid_g[own, HD:])
        k = jnp.concatenate(
            [mid_ref[p * 256 + j * 128 : p * 256 + (j + 1) * 128, :HD] for p in range(4)], 0
        )
        v = jnp.concatenate(
            [mid_ref[p * 256 + j * 128 : p * 256 + (j + 1) * 128, HD : 2 * HD] for p in range(4)], 0
        )
        s = jnp.where(keep, dot_nt(q, k) * SCALE, NEG)
        p = jnp.exp(s - lse)
        ds = (p * (dot_nt(g, v) - delta)).astype(BF)
        fs = far_scr.at[j]
        fs[...] = dot_nn(ds, k) * SCALE
        spread = pl.ds(head // 8, 8, stride=16)
        fs[spread, :] = fs[spread, :] + far_dq[j * 8 : (j + 1) * 8]
        picked = pl.ds(lax.rem(head, 8), 128, stride=8)
        sc = scr.at[j]
        sc[:SEG, :], sc[SEG:, :] = dq0[j], dq1[j]
        sc[picked, :] = sc[picked, :] + fs[...]
        out_ref[:, j * HD : (j + 1) * HD] = sc[...].astype(BF)


def stat_rows(packs):
    lane, row = iota((8, HD), 1), iota((8, HD), 0)
    pick = ((row == lane // 3) & (lane < 6)).astype(F32).astype(BF)
    stats = dot_nt(pick, packs)
    return stats[0:1], stats[1:2]


def far_key_kernel(idx, far_all, grads, dq_ref, out_ref):
    @pl.when((idx[0] & 1) == 0)
    def _():
        lse, delta = stat_rows(grads[:, HD : 2 * HD])
        k, v = far_all[:32, :HD], far_all[:32, HD : 2 * HD]
        q_all, g_all = grads[:, 2 * HD :], grads[:, :HD]
        s = jnp.where(far_keep_backward(idx[0]), dot_nt(k, q_all) * SCALE, NEG)
        p = jnp.exp(s - lse)
        ds = (p * (dot_nt(v, g_all) - delta)).astype(BF)
        out_ref[:32, :] = dot_nn(ds, q_all) * SCALE
        out_ref[32:64, :] = dot_nn(p.astype(BF), g_all)
        out_ref[64:, :] = dq_ref[...]


def mid_key_kernel(idx, dk0, dk1, dv0, dv1, mid_ref, grads, dk_ref, dv_ref):
    s_idx = idx[0]
    all_lse, all_delta = stat_rows(grads[:, HD:])
    query_slot = mid_slots(s_idx, (128, SEG), 1)
    key_slot = (s_idx & 3) * 128 + iota((128, SEG), 0)
    keep = key_slot <= query_slot
    for j in range(2):
        own = slice(j * 128, (j + 1) * 128)
        places = [slice(p * 256 + j * 128, p * 256 + (j + 1) * 128) for p in range(4)]
        k, v = mid_ref[own, :HD], mid_ref[own, HD : 2 * HD]
        q = jnp.concatenate([mid_ref[r, 2 * HD :] for r in places], 0)
        g = jnp.concatenate([grads[r, :HD] for r in places], 0)
        lse = jnp.concatenate([all_lse[:, r] for r in places], 1)
        delta = jnp.concatenate([all_delta[:, r] for r in places], 1)
        s = jnp.where(keep, dot_nt(k, q) * SCALE, NEG)
        p = jnp.exp(s - lse)
        ds = (p * (dot_nt(v, g) - delta)).astype(BF)
        picked = pl.ds(lax.rem(idx[1] * 2 + j, 8), 128, stride=8)
        for near0, near1, mid, out_ref in (
            (dk0, dk1, dot_nn(ds, q) * SCALE, dk_ref),
            (dv0, dv1, dot_nn(p.astype(BF), g), dv_ref),
        ):
            out = out_ref.at[j]
            out[:SEG, :], out[SEG:, :] = near0[j], near1[j]
            out[picked, :] = out[picked, :] + mid


def key_grad_kernel(idx, dk_in, dv_in, far_got, far_own, dk_out, dv_out, whole_ref):
    row = iota((128, HD), 0)
    for j in range(2):
        here = row == idx[1] * 2 + j
        cols = slice(j * HD, (j + 1) * HD)
        for a, (near, out) in enumerate(((dk_in, dk_out), (dv_in, dv_out))):
            first = a * 32 + j * 8
            far = by_parity(idx, far_got[first : first + 8], far_own[first + 16 : first + 24])
            whole_ref[a, :, cols] = far
            for b in range(8):
                rows = slice(b * 128, (b + 1) * 128)
                total = near[j, rows, :] + jnp.where(here, far[b : b + 1], 0.0)
                out[rows, cols] = total.astype(BF)


def exchange(x, bit):
    return lax.ppermute(x, "seq", [(i, i ^ bit) for i in range(64)])


def chip_exchange(x, bit, parity):
    return lax.ppermute(x, "seq", [(i, i ^ bit) for i in range(parity, 64, 2)])


def head_exchange(x, bit, parity):
    pairs = [(s * 8 + h, s * 8 + (h ^ bit)) for s in range(parity, 64, 2) for h in range(8)]
    return lax.ppermute(x, ("seq", "head"), pairs)


def to_odd(x):
    return lax.ppermute(x, "seq", [(i, i + 1) for i in range(0, 64, 2)])


def to_even(x):
    return lax.ppermute(x, "seq", [(i + 1, i) for i in range(0, 64, 2)])


def joined(a, b):
    return jnp.concatenate([a, b], 0)


def after(arrays):
    return lax.optimization_barrier(arrays)


def sds(shape, dtype):
    return jax.ShapeDtypeStruct(shape, dtype)


def local(queries, keys, values, out_grad):
    seq_index = lax.axis_index("seq")
    head_index = lax.axis_index("head")
    idx = jnp.stack([seq_index, head_index]).astype(jnp.int32)

    mid0, far0 = pl.pallas_call(
        select_kernel,
        out_shape=(sds((256, 384), BF), sds((16, 384), BF)),
        in_specs=[SMEM, VMEM, VMEM, VMEM],
        out_specs=(VMEM, VMEM),
        scratch_shapes=[pltpu.VMEM((6, TOK, HD), F32)],
        compiler_params=PARAMS,
        cost_estimate=cost(10**6, 2 * 10**6),
        name="select",
    )(idx, queries, keys, values)

    unit = pl.BlockSpec((SEG, HD), lambda b, j: (b, j))
    by_head = pl.BlockSpec((1, SEG, HD), lambda b, j: (j, b, 0))
    by_head_shape = sds((2, TOK, HD), F32)
    half = pl.BlockSpec((1, SEG, HD), lambda j: (j, 0, 0))
    half_shape = sds((2, SEG, HD), F32)

    def near_forward(block):
        part = pl.BlockSpec((SEG, HD), lambda j: (block, j))
        return pl.pallas_call(
            near_forward_kernel,
            grid=(2,),
            out_shape=(half_shape, half_shape),
            in_specs=[part, part, part],
            out_specs=(half, half),
            compiler_params=PARAMS,
            cost_estimate=cost(4 * 10**8, 2 * 10**6, 10**6),
            name=f"near_forward_{block}",
        )(queries, keys, values)

    mid1 = exchange(mid0, 2)
    mate_far = to_odd(far0)
    near0, near1 = near_forward(0), near_forward(1)
    mid_two, far1, near0, near1 = after(
        (joined(mid0, mid1), joined(far0, mate_far), near0, near1)
    )
    mid2 = exchange(mid_two, 1)
    mid_all = joined(mid_two, mid2)
    mid_o, mid_lse = pl.pallas_call(
        mid_forward_kernel,
        out_shape=(sds((256, HD), F32), sds((256, HD), F32)),
        in_specs=[SMEM, VMEM],
        out_specs=(VMEM, VMEM),
        compiler_params=PARAMS,
        cost_estimate=cost(2 * 10**8, 10**6, 10**5),
        name="mid_forward",
    )(idx, mid_all)

    att, lse12, bundle = pl.pallas_call(
        pre_kernel,
        out_shape=(sds((TOK, 256), BF), by_head_shape, sds((80, HD), F32)),
        in_specs=[SMEM] + [VMEM] * 7,
        out_specs=(VMEM,) * 3,
        scratch_shapes=[pltpu.VMEM((2, TOK, HD), F32)],
        compiler_params=PARAMS,
        cost_estimate=cost(10**7, 4 * 10**6, 10**5),
        name="pre",
    )(idx, *near0, *near1, mid_o, mid_lse, out_grad)
    rows, bundle = after((far1, bundle))
    far1 = rows[:, : 2 * HD]
    mate_stats = to_even(bundle[48:])
    from1 = chip_exchange(far1, 32, 1)
    stats = joined(mate_stats, bundle[48:])
    sums1 = head_exchange(stats, 2, 0)
    far2, stats = after((joined(far1, from1), stats + sums1))
    from2 = chip_exchange(far2, 16, 1)
    sums2 = head_exchange(stats, 1, 0)
    far4, stats = after((joined(far2, from2), stats + sums2))
    from4 = chip_exchange(far4, 8, 1)
    sums3 = head_exchange(stats, 4, 0)
    far8 = joined(far4, from4)
    from8 = chip_exchange(far8, 4, 1)
    far16 = joined(far8, from8)
    from16 = chip_exchange(far16, 2, 1)
    stats = stats + sums3
    mate = to_odd(joined(bundle[:48], stats))
    far_all = joined(far16, from16)
    far_all, mate = after((far_all, mate))
    far_even = to_even(far_all)

    packs, fix = pl.pallas_call(
        far_kernel,
        out_shape=(sds((64, 384), BF), sds((8, HD), F32)),
        in_specs=[SMEM] + [VMEM] * 4,
        out_specs=(VMEM,) * 2,
        scratch_shapes=[pltpu.VMEM((4, 64, HD), F32)],
        compiler_params=PARAMS,
        cost_estimate=cost(10**7, 10**6, 10**5),
        name="far",
    )(idx, far_all, rows, bundle, mate)

    packs_even = to_even(packs)
    fix1 = head_exchange(fix, 2, 1)
    part0, fix = after((packs_even[:32], fix + fix1))
    part1 = chip_exchange(part0, 32, 0)
    fix2 = head_exchange(fix, 1, 1)
    part_a, fix = after((joined(part0, part1), fix + fix2))
    part2 = chip_exchange(part_a, 16, 0)
    fix3 = head_exchange(fix, 4, 1)
    far_dq = pl.pallas_call(
        far_query_kernel,
        out_shape=sds((32, HD), F32),
        in_specs=[SMEM] + [VMEM] * 2,
        out_specs=VMEM,
        compiler_params=PARAMS,
        cost_estimate=cost(10**7, 10**6, 10**5),
        name="far_query",
    )(idx, far_even, packs_even)
    part_b, fix = after((joined(part_a, part2), fix + fix3))
    part3 = chip_exchange(part_b, 8, 0)
    part_b, far_dq = after((part_b, far_dq))
    part_c = joined(part_b, part3)
    part4 = chip_exchange(part_c, 4, 0)
    part_c, fix_sent = after((part_c, fix))
    fix_even = to_even(fix_sent)
    normed, grad, delta, lse, mid_g = pl.pallas_call(
        norm_kernel,
        out_shape=(
            sds((TOK, 256), BF),
            sds((TOK, 256), BF),
            by_head_shape,
            by_head_shape,
            sds((256, 256), BF),
        ),
        in_specs=[SMEM] + [VMEM] * 9,
        out_specs=(VMEM,) * 5,
        scratch_shapes=[pltpu.VMEM((2, TOK, HD), F32), pltpu.VMEM((32, HD), F32)],
        compiler_params=PARAMS,
        cost_estimate=cost(10**7, 4 * 10**6),
        name="norm",
    )(idx, mate, stats, fix, fix_even, packs, packs_even, att, out_grad, lse12)

    def near_backward(block):
        part = pl.BlockSpec((SEG, HD), lambda j: (block, j))
        stat = pl.BlockSpec((1, SEG, HD), lambda j: (j, block, 0))
        return pl.pallas_call(
            near_backward_kernel,
            grid=(2,),
            out_shape=(half_shape,) * 3,
            in_specs=[part] * 4 + [stat] * 2,
            out_specs=(half,) * 3,
            compiler_params=PARAMS,
            cost_estimate=cost(10**9, 4 * 10**6, 10**6),
            name=f"near_backward_{block}",
        )(queries, keys, values, grad, lse, delta)

    mid_g1 = exchange(mid_g, 2)
    part_d, grad = after((joined(part_c, part4), grad))
    part5 = chip_exchange(part_d, 2, 0)
    dq0, dk0, dv0 = near_backward(0)
    dq1, dk1, dv1 = near_backward(1)
    mid_gs, far_gs, dq0, dq1 = after(
        (joined(mid_g, mid_g1), joined(part_d, part5), dq0, dq1)
    )
    mid_g2 = exchange(mid_gs, 1)

    far_kv = pl.pallas_call(
        far_key_kernel,
        out_shape=sds((96, HD), F32),
        in_specs=[SMEM] + [VMEM] * 3,
        out_specs=VMEM,
        compiler_params=PARAMS,
        cost_estimate=cost(10**7, 10**6, 10**5),
        name="far_key",
    )(idx, far_even, far_gs, far_dq)
    mate_kv = to_odd(far_kv)

    mid_gall = joined(mid_gs, mid_g2)
    dk, dv = pl.pallas_call(
        mid_key_kernel,
        out_shape=(by_head_shape, by_head_shape),
        in_specs=[SMEM] + [VMEM] * 6,
        out_specs=(VMEM,) * 2,
        compiler_params=PARAMS,
        cost_estimate=cost(2 * 10**8, 4 * 10**6, 10**5),
        name="mid_key",
    )(idx, dk0, dk1, dv0, dv1, mid_all, mid_gall)
    mate_kv, dk = after((mate_kv, dk))

    grad_queries = pl.pallas_call(
        query_grad_kernel,
        out_shape=sds((TOK, 256), BF),
        in_specs=[SMEM] + [VMEM] * 6,
        out_specs=VMEM,
        scratch_shapes=[pltpu.VMEM((2, TOK, HD), F32), pltpu.VMEM((2, 128, HD), F32)],
        compiler_params=PARAMS,
        cost_estimate=cost(2 * 10**8, 3 * 10**6, 10**5),
        name="query_grad",
    )(idx, dq0, dq1, mid_all, mid_g, mate_kv, far_kv)

    grad_keys, grad_values, whole = pl.pallas_call(
        key_grad_kernel,
        out_shape=(sds((TOK, 256), BF), sds((TOK, 256), BF), sds((2, 8, 256), F32)),
        in_specs=[SMEM] + [VMEM] * 4,
        out_specs=(VMEM,) * 3,
        compiler_params=PARAMS,
        cost_estimate=cost(10**6, 4 * 10**6),
        name="key_grad",
    )(idx, dk, dv, mate_kv, far_kv)

    return normed, grad_queries, grad_keys, grad_values, whole


def solution(mesh):
    spec = P("seq", "head")
    return jax.shard_map(
        local,
        mesh=mesh,
        in_specs=(spec,) * 4,
        out_specs=(spec,) * 4 + (P(None, "seq", "head"),),
        check_vma=False,
    )
```
